512 devices in a mesh: band: 32 (over z, x_lo), member: 16 (over y, x_hi, core).
Axes of the slice: x: 4 (x_hi: 2, x_lo: 2; x = x_hi * 2 + x_lo), y: 4, z: 16, core: 2. Of those that a mesh axis runs over, the one named last changes fastest.
Arguments:
- tracer_mean: float32 [16, 4, 256, 768], P('member', None, 'band'), may hold values from -6 to 6
- slope_lon: float32 [16, 4, 256, 768], P('member', None, 'band'), may hold values from -3 to 3
- slope_lat: float32 [16, 4, 256, 768], P('member', None, 'band'), may hold values from -3 to 3
- zonal_courant: float32 [16, 4, 256, 768], P('member', None, 'band'), may hold values from -0.6 to 0.6
- merid_courant: float32 [16, 4, 256, 768], P('member', None, 'band'), may hold values from -0.6 to 0.6
- mixing: float32 [3, 256, 768], P(None, 'band'), may hold values from 0.1 to 3
- flux_map: float32 [256, 768], P('band'), may hold values from -6 to 6
- region: int32 [256, 768], P('band'), may hold values from 0 to 21
- scaling: float32 [16, 22], P('member'), may hold values from 0.5 to 2
- reader: int32 [32], P('band'), may hold values from 0 to 15
Outputs:
- new_mean: float32 [16, 4, 256, 768], P('member', None, 'band')
- new_slope_lon: float32 [16, 4, 256, 768], P('member', None, 'band')
- new_slope_lat: float32 [16, 4, 256, 768], P('member', None, 'band')
The draws below stay inside these ranges and needn't reach their ends.
All inputs are finite; a program needn't handle non-finite values.
Results may differ from the reference program's by a relative error of at most 0.0003.
Values sent between devices are 32-bit elements; how exact they have to be, the bound alone decides.
A program may use at most 64 MiB of HBM per device.

```python
import math
import jax
import jax.numpy as jnp
from jax import lax

LEV = 4
LON = 768
REGIONS = 22
SUB = 2
LAT = 256
TRACERS = 16
N_BAND = 32
N_MEMBER = 16


def plant(array, stream_key, least, largest):
    longest = array.shape.index(max(array.shape))
    spots = []
    for shift in (0, 1):
        where = [jax.random.randint(jax.random.fold_in(stream_key, axis), (), 0, length) for axis, length in enumerate(array.shape)]
        where[longest] = (where[longest] + shift) % array.shape[longest]
        spots.append(tuple(where))
    return array.at[spots[0]].set(least).at[spots[1]].set(largest)


def level_of(rng, shape, split, least, top_value):
    level = 1.0
    for dim, shards_of in split:
        heights = jax.random.uniform(jax.random.fold_in(jax.random.fold_in(rng, 6), dim), (shards_of,), jnp.float32, least / len(split), top_value / len(split))
        level = level * jnp.repeat(jnp.exp(heights), shape[dim] // shards_of).reshape((-1,) + (1,) * (len(shape) - 1 - dim))
    return level


def bell_draw(own_key, dims, deviation, reach, pieces=(), kind=jnp.bfloat16):
    gain = level_of(own_key, dims, pieces, -0.22, 0.18) if pieces else 1.0
    values = jax.random.normal(own_key, dims, jnp.float32) * deviation * gain
    return jnp.minimum(jnp.maximum(values, -reach), reach).astype(kind)


def setup_inputs(seed: int = 0) -> dict:
    keys = jax.random.split(jax.random.key(seed), 11)
    return {
        "tracer_mean": bell_draw(keys[0], (TRACERS, LEV, LAT, LON), 1.0, 6.0, ((0, 16), (2, 32)), jnp.float32),
        "slope_lon": bell_draw(keys[1], (TRACERS, LEV, LAT, LON), 0.5, 3.0, ((0, 16), (2, 32)), jnp.float32),
        "slope_lat": bell_draw(keys[2], (TRACERS, LEV, LAT, LON), 0.5, 3.0, ((0, 16), (2, 32)), jnp.float32),
        "zonal_courant": jnp.clip(jax.random.uniform(keys[3], (N_MEMBER, LEV, LAT, LON), jnp.float32, -0.6, 0.6) * level_of(keys[3], (N_MEMBER, LEV, LAT, LON), ((0, 16), (2, 32)), -0.4, 0.0), -0.6, 0.6),
        "merid_courant": jnp.clip(jax.random.uniform(keys[4], (N_MEMBER, LEV, LAT, LON), jnp.float32, -0.6, 0.6) * level_of(keys[4], (N_MEMBER, LEV, LAT, LON), ((0, 16), (2, 32)), -0.4, 0.0), -0.6, 0.6),
        "mixing": jnp.clip(jnp.exp(math.log(3.0) - 3.4011974 * jax.random.uniform(keys[5], (LEV - 1, LAT, LON), jnp.float32) ** level_of(keys[5], (LEV - 1, LAT, LON), ((1, 32),), -0.2, 0.2)), 0.1, 3.0),
        "flux_map": bell_draw(keys[6], (LAT, LON), 1.0, 6.0, ((0, 32),), jnp.float32),
        "region": plant(jax.random.randint(keys[7], (LAT, LON), 0, REGIONS), jax.random.fold_in(keys[7], 1), 0, REGIONS - 1).astype(jnp.int32),
        "scaling": jnp.clip(jnp.exp(math.log(2.0) - 1.3862944 * jax.random.uniform(keys[8], (TRACERS, REGIONS), jnp.float32) ** level_of(keys[8], (TRACERS, REGIONS), ((0, 16),), -0.2, 0.2)), 0.5, 2.0),
        "reader": plant(jax.random.randint(keys[9], (N_BAND,), 0, N_MEMBER), jax.random.fold_in(keys[9], 1), 0, N_MEMBER - 1).astype(jnp.int32),
    }


def window(field, start, size, axis):
    return lax.slice_in_dim(field, start, start + size, axis=axis)


def sweep(mean_ext, along_ext, cross_ext, faces, axis):
    count = mean_ext.shape[axis] - 2
    left_mean = window(mean_ext, 0, count + 1, axis)
    right_mean = window(mean_ext, 1, count + 1, axis)
    left_along = window(along_ext, 0, count + 1, axis)
    right_along = window(along_ext, 1, count + 1, axis)
    left_cross = window(cross_ext, 0, count + 1, axis)
    right_cross = window(cross_ext, 1, count + 1, axis)
    forward = faces > 0.0
    flux = jnp.where(forward, faces * (left_mean + 0.5 * (1.0 - faces) * left_along),
                     faces * (right_mean - 0.5 * (1.0 + faces) * right_along))
    along_flux = faces * jnp.where(forward, left_along, right_along)
    cross_flux = faces * jnp.where(forward, left_cross, right_cross)

    def divergence(values):
        return window(values, 0, count, axis) - window(values, 1, count, axis)

    new_mean = window(mean_ext, 1, count, axis) + divergence(flux)
    new_along = 0.5 * (window(along_ext, 1, count, axis) + divergence(along_flux)) + 0.25 * (
        window(mean_ext, 2, count, axis) - window(mean_ext, 0, count, axis))
    new_cross = window(cross_ext, 1, count, axis) + divergence(cross_flux)
    return new_mean, new_along, new_cross


def extend_cycle(field):
    return jnp.concatenate([field[..., -1:], field, field[..., :1]], -1)


def extend_edge(field):
    return jnp.concatenate([field[..., :1, :], field, field[..., -1:, :]], -2)


def zonal_sweep(mean, along, cross, uwind):
    faces = jnp.concatenate([uwind, uwind[..., :1]], -1)
    return sweep(extend_cycle(mean), extend_cycle(along), extend_cycle(cross), faces, -1)


def vertical_mix(fields, mixing):
    levels = fields.shape[-3]
    zero = jnp.zeros_like(mixing[0])
    below = [zero] + [mixing[level - 1] for level in range(1, levels)]
    above = [mixing[level] for level in range(levels - 1)] + [zero]
    ratios = []
    values = []
    for level in range(levels):
        source = fields[..., level, :, :]
        denom = 1.0 + below[level] + above[level]
        if level > 0:
            denom = denom + below[level] * ratios[-1]
            source = source + below[level] * values[-1]
        ratios.append(-above[level] / denom)
        values.append(source / denom)
    result = [values[-1]]
    for level in range(levels - 2, -1, -1):
        result.append(values[level] - ratios[level] * result[-1])
    ordered = result[::-1]
    return jnp.stack(ordered, axis=-3)


def emission_of(flux_map, region, scaling):
    count = scaling.shape[-1]
    region_codes = jnp.arange(count, dtype=jnp.int32)
    onehot = (region[None] == region_codes[:, None, None]).astype(jnp.float32)
    weight = jnp.tensordot(scaling, onehot, axes=1, precision=lax.Precision.HIGHEST)
    land = jnp.where(region < count // 2, 1.0, 0.4)
    return 0.5 * flux_map * land * weight


def pick_slab(met, reader):
    bands = reader.shape[0]
    blocks = met.reshape(met.shape[0], met.shape[1], bands, -1, met.shape[3])
    chosen = blocks[reader, :, jnp.arange(bands, dtype=jnp.int32)]
    return jnp.transpose(chosen, (1, 0, 2, 3)).reshape(met.shape[1], -1, met.shape[3])


def reference(tracer_mean, slope_lon, slope_lat, zonal_courant, merid_courant, mixing, flux_map, region, scaling, reader):
    uwind = pick_slab(zonal_courant, reader)
    vwind = pick_slab(merid_courant, reader)
    rows_all = jnp.arange(vwind.shape[1], dtype=jnp.int32)[None, :, None]
    vwind = jnp.where(rows_all > 0, vwind, jnp.float32(0.0))
    mean = tracer_mean.at[:, 0].add(emission_of(flux_map, region, scaling))
    fields = vertical_mix(jnp.stack([mean, slope_lon, slope_lat]), mixing)
    mean, along_lon, along_lat = fields[0], fields[1], fields[2]
    faces = jnp.concatenate([vwind, jnp.zeros_like(vwind[:, :1])], 1)
    for substep in range(SUB):
        mean, along_lon, along_lat = zonal_sweep(mean, along_lon, along_lat, uwind)
        mean, along_lat, along_lon = sweep(extend_edge(mean), extend_edge(along_lat), extend_edge(along_lon), faces, -2)
    return mean, along_lon, along_lat
```

```python
import jax
import jax.numpy as jnp
from jax import lax
from jax.experimental import pallas as pl
from jax.experimental.pallas import tpu as pltpu
from jax.sharding import PartitionSpec as P

SUB = 2
MESH = pl.DeviceIdType.MESH
LEVELS, ROWS, LONS = 4, 8, 768
MEMBERS, CHIPS, HALF = 16, 8, 384


def upwind(faces, left, right):
    forward = faces > 0.0
    mean, along, cross = (jnp.where(forward, l, r) for l, r in zip(left, right))
    weight = 0.5 * (jnp.where(forward, 1.0, -1.0) - faces)
    return faces * (mean + weight * along), faces * along, faces * cross


def advance(cells, flux, flux_next, mean_prev, mean_next):
    mean, along, cross = cells
    return (
        mean + (flux[0] - flux_next[0]),
        0.5 * (along + (flux[1] - flux_next[1])) + 0.25 * (mean_next - mean_prev),
        cross + (flux[2] - flux_next[2]),
    )


def zonal(cells, faces):
    count = faces.shape[-1]
    left = tuple(pltpu.roll(x, 1, 1) for x in cells)
    flux = upwind(faces, left, cells)
    flux_next = tuple(pltpu.roll(x, count - 1, 1) for x in flux)
    return advance(cells, flux, flux_next, left[0], pltpu.roll(cells[0], count - 1, 1))


def kernel(
    mean_h, lon_h, lat_h, zon_h, mer_h, mix_h, flux_h, region_h, scaling_s, reader_s,
    out_mean, out_lon, out_lat,
    cells, mix_v, flux_v, region_v, got, winds, pack, halo, edge,
    in_sem, own_sem, scatter_send, scatter_recv, gather_send, gather_recv,
    halo_send, halo_recv, out_sem,
):
    band, me = lax.axis_index("band"), lax.axis_index("member")
    bands = lax.axis_size("band")
    chip, core = me // 2, me % 2
    has_south, has_north = band > 0, band < bands - 1

    loads = [
        pltpu.make_async_copy(mix_h, mix_v, in_sem.at[3]),
        pltpu.make_async_copy(flux_h, flux_v, in_sem.at[4]),
        pltpu.make_async_copy(region_h, region_v, in_sem.at[5]),
        pltpu.make_async_copy(mean_h.at[0], cells.at[0], in_sem.at[0]),
        pltpu.make_async_copy(lon_h.at[0], cells.at[1], in_sem.at[1]),
        pltpu.make_async_copy(lat_h.at[0], cells.at[2], in_sem.at[2]),
    ]
    for load in loads:
        load.start()

    barrier = pltpu.get_barrier_semaphore()
    for step in range(1, MEMBERS):
        pl.semaphore_signal(barrier, inc=1, device_id=(band, (me + step) % MEMBERS), device_id_type=MESH)

    @pl.when(has_south)
    def _():
        pl.semaphore_signal(barrier, inc=1, device_id=(band - 1, me), device_id_type=MESH)

    @pl.when(has_north)
    def _():
        pl.semaphore_signal(barrier, inc=1, device_id=(band + 1, me), device_id_type=MESH)

    pl.semaphore_wait(barrier, MEMBERS - 1 + has_south.astype(jnp.int32) + has_north.astype(jnp.int32))

    def piece(c, q):
        source = mer_h if c else zon_h
        return source.at[0, q // 2, :, pl.ds(pl.multiple_of((q % 2) * HALF, HALF), HALF)]

    for c in range(2):
        for d in range(CHIPS):
            q = (chip + d) % CHIPS
            slot = (2 * d + c - core + MEMBERS) % MEMBERS

            def send():
                pltpu.make_async_remote_copy(
                    src_ref=piece(c, q), dst_ref=got.at[slot], send_sem=scatter_send,
                    recv_sem=scatter_recv, device_id=(band, 2 * q + c), device_id_type=MESH,
                ).start()

            if d:
                send()
            else:
                pl.when(core != c)(send)

                @pl.when(core == c)
                def _():
                    pltpu.make_async_copy(piece(c, q), got.at[0], own_sem).start()

    for load in loads[:3]:
        load.wait()
    region = region_v[...]
    weight = jnp.zeros(region.shape, jnp.float32)
    for code in range(scaling_s.shape[1]):
        weight = jnp.where(region == code, scaling_s[0, code], weight)
    land = jnp.where(region < scaling_s.shape[1] // 2, 1.0, 0.4)
    emission = 0.5 * flux_v[...] * land * weight
    zero = jnp.zeros_like(emission)
    below = [zero] + [mix_v[level] for level in range(LEVELS - 1)]
    above = below[1:] + [zero]
    ratios, inverse = [], []
    for level in range(LEVELS):
        denom = 1.0 + below[level] + above[level]
        if level:
            denom = denom + below[level] * ratios[-1]
        inverse.append(1.0 / denom)
        ratios.append(-above[level] * inverse[-1])
    for load in loads[3:]:
        load.wait()
    for k in range(3):
        values = []
        for level in range(LEVELS):
            source = cells[k, level]
            if k == 0 and level == 0:
                source = source + emission
            if level:
                source = source + below[level] * values[-1]
            values.append(source * inverse[level])
        result = values[-1]
        cells[k, LEVELS - 1] = result
        for level in range(LEVELS - 2, -1, -1):
            result = values[level] - ratios[level] * result
            cells[k, level] = result

    pltpu.make_async_copy(piece(0, chip), got.at[0], own_sem).wait()
    rest = got.at[pl.ds(1, MEMBERS - 1)]
    pltpu.make_async_copy(rest, rest, scatter_recv).wait()
    winds[core, chip] = got[(me - reader_s[0] + MEMBERS) % MEMBERS]
    for step in range(1, MEMBERS):
        pltpu.make_async_remote_copy(
            src_ref=winds.at[core, chip], dst_ref=winds.at[core, chip], send_sem=gather_send,
            recv_sem=gather_recv.at[core], device_id=(band, (me + step) % MEMBERS), device_id_type=MESH,
        ).start()

    def await_winds(c):
        for count in (CHIPS - 1, CHIPS):
            @pl.when((core == c) == (count == CHIPS - 1))
            def _():
                part = winds.at[c, pl.ds(0, count)]
                pltpu.make_async_copy(part, part, gather_recv.at[c]).wait()

    def wind(c, level):
        return jnp.concatenate([winds[c, 2 * level], winds[c, 2 * level + 1]], -1)

    row = lax.broadcasted_iota(jnp.int32, (ROWS, LONS), 0)
    outs = (out_mean, out_lon, out_lat)

    for sub in range(SUB):
        if sub == 0:
            await_winds(0)
        for level in range(LEVELS):
            new = zonal((cells[0, level], cells[1, level], cells[2, level]), wind(0, level))
            for k in range(3):
                cells[k, level] = new[k]
                for side, r in ((0, 0), (1, ROWS - 1)):
                    pack[sub, side, pl.ds(k * LEVELS + level, 1), :] = new[k][r:r + 1]
        if sub == 0:
            await_winds(1)
        for level in range(LEVELS):
            v = wind(1, level)
            pack[sub, 0, pl.ds(3 * LEVELS + level, 1), :] = v[0:1]
            pack[sub, 1, pl.ds(3 * LEVELS + level, 1), :] = jnp.zeros((1, LONS), jnp.float32)

        def exchange(side):
            return pltpu.make_async_remote_copy(
                src_ref=pack.at[sub, side], dst_ref=halo.at[sub, 1 - side],
                send_sem=halo_send.at[sub, side], recv_sem=halo_recv.at[sub, 1 - side],
                device_id=(band + (1 if side else -1), me), device_id_type=MESH,
            )

        for side, there in ((0, has_south), (1, has_north)):
            pl.when(there)(exchange(side).start)

        for side, there in ((0, has_south), (1, has_north)):
            @pl.when(there)
            def _():
                exchange(1 - side).wait_recv()

            @pl.when(jnp.logical_not(there))
            def _():
                halo[sub, side] = pack[sub, side]
                halo[sub, side, pl.ds(3 * LEVELS, LEVELS), :] = jnp.zeros((LEVELS, LONS), jnp.float32)

        def packed(ref, side):
            return tuple(ref[sub, side, pl.ds(k * LEVELS, LEVELS), :] for k in (0, 2, 1))

        last = upwind(halo[sub, 1, pl.ds(3 * LEVELS, LEVELS), :], packed(pack, 1), packed(halo, 1))
        for k in range(3):
            edge[k] = last[k]

        for level in range(LEVELS):
            faces = wind(1, level)
            faces = jnp.where(jnp.logical_and(row == 0, band == 0), 0.0, faces)
            here = tuple(cells[k, level] for k in (0, 2, 1))
            south = [halo[sub, 0, pl.ds(k * LEVELS + level, 1), :] for k in (0, 2, 1)]
            left = tuple(
                jnp.where(row == 0, s, pltpu.roll(x, 1, 0)) for s, x in zip(south, here)
            )
            flux = upwind(faces, left, here)
            flux_next = tuple(
                jnp.where(row == ROWS - 1, edge[k, pl.ds(level, 1), :], pltpu.roll(flux[k], ROWS - 1, 0))
                for k in range(3)
            )
            mean_next = jnp.where(
                row == ROWS - 1, halo[sub, 1, pl.ds(level, 1), :], pltpu.roll(here[0], ROWS - 1, 0)
            )
            new = advance(here, flux, flux_next, left[0], mean_next)
            for k, value in zip((0, 2, 1), new):
                cells[k, level] = value

    stores = [pltpu.make_async_copy(cells.at[k], outs[k].at[0], out_sem.at[k]) for k in range(3)]
    for store in stores:
        store.start()
    pltpu.make_async_copy(rest, rest, scatter_send).wait()
    sent = got.at[pl.ds(1, MEMBERS - 1)]
    pltpu.make_async_copy(sent, sent, gather_send).wait()
    for sub in range(SUB):
        for side, there in ((0, has_south), (1, has_north)):
            @pl.when(there)
            def _():
                done = pack.at[sub, side]
                pltpu.make_async_copy(done, done, halo_send.at[sub, side]).wait()
    for store in stores:
        store.wait()


def on_device(*args):
    shape = jax.ShapeDtypeStruct(args[0].shape, jnp.float32)
    hbm = pl.BlockSpec(memory_space=pl.ANY)
    smem = pl.BlockSpec(memory_space=pltpu.SMEM)
    dma = pltpu.SemaphoreType.DMA
    vmem = lambda *dims: pltpu.VMEM(dims, jnp.float32)
    return pl.pallas_call(
        kernel,
        out_shape=(shape,) * 3,
        in_specs=[hbm] * 8 + [smem] * 2,
        out_specs=(hbm,) * 3,
        scratch_shapes=[
            vmem(3, LEVELS, ROWS, LONS),
            vmem(LEVELS - 1, ROWS, LONS),
            vmem(ROWS, LONS),
            pltpu.VMEM((ROWS, LONS), jnp.int32),
            vmem(MEMBERS, ROWS, HALF),
            vmem(2, CHIPS, ROWS, HALF),
            vmem(SUB, 2, 4 * LEVELS, LONS),
            vmem(SUB, 2, 4 * LEVELS, LONS),
            vmem(3, LEVELS, LONS),
            dma((6,)), dma, dma, dma, dma, dma((2,)), dma((SUB, 2)), dma((SUB, 2)), dma((3,)),
        ],
        compiler_params=pltpu.CompilerParams(collective_id=0, has_side_effects=True),
    )(*args)


def solution(mesh):
    moments = P("member", None, "band", None)
    return jax.shard_map(
        on_device,
        mesh=mesh,
        in_specs=(
            moments, moments, moments, moments, moments,
            P(None, "band", None),
            P("band", None),
            P("band", None),
            P("member", None),
            P("band"),
        ),
        out_specs=(moments,) * 3,
        check_vma=False,
    )
```

```python
import jax
import jax.numpy as jnp
from jax import lax
from jax.experimental import pallas as pl
from jax.experimental.pallas import tpu as pltpu
from jax.sharding import PartitionSpec as P

SUB = 2
MESH = pl.DeviceIdType.MESH
LEVELS, ROWS, LONS, REGIONS = 4, 8, 768, 22
MEMBERS, CHIPS, HALF = 16, 8, 384
U, V = 3, 4
OFFSETS = ((2, 1), (1, 1), (3, 1), (2, 0), (0, 1), (1, 0), (3, 0), (0, 0))


def upwind(faces, left, right):
    forward = faces > 0.0
    mean, along, cross = (jnp.where(forward, l, r) for l, r in zip(left, right))
    weight = 0.5 * (jnp.where(forward, 1.0, -1.0) - faces)
    return faces * (mean + weight * along), faces * along, faces * cross


def advance(cells, flux, flux_next, mean_prev, mean_next):
    mean, along, cross = cells
    return (
        mean + (flux[0] - flux_next[0]),
        0.5 * (along + (flux[1] - flux_next[1])) + 0.25 * (mean_next - mean_prev),
        cross + (flux[2] - flux_next[2]),
    )


def zonal(cells, faces):
    count = faces.shape[-1]
    left = tuple(pltpu.roll(x, 1, 1) for x in cells)
    flux = upwind(faces, left, cells)
    flux_next = tuple(pltpu.roll(x, count - 1, 1) for x in flux)
    return advance(cells, flux, flux_next, left[0], pltpu.roll(cells[0], count - 1, 1))


def wind_of(winds, c, level):
    return jnp.concatenate([winds[c, 2 * level], winds[c, 2 * level + 1]], -1)


def exchange_kernel(
    mean_h, lon_h, lat_h, zon_h, mer_h, mix_h, flux_h, region_h, scaling_h, reader_h,
    cells, winds, halo,
    mix_v, flux_v, region_v, scaling_s, reader_s, got, pack,
    in_sem, own_sem, scatter_send, scatter_recv, gather_send, gather_recv,
    halo_send, halo_recv, late, beside,
):
    band, me = lax.axis_index("band"), lax.axis_index("member")
    bands = lax.axis_size("band")
    chip, core = me // 2, me % 2
    has_south, has_north = band > 0, band < bands - 1
    around = has_south.astype(jnp.int32) + has_north.astype(jnp.int32)
    tail_end = me == 0
    answers = jnp.logical_and(tail_end, band % 2 == 0)

    loads = [
        pltpu.make_async_copy(mix_h, mix_v, in_sem.at[3]),
        pltpu.make_async_copy(flux_h, flux_v, in_sem.at[4]),
        pltpu.make_async_copy(region_h, region_v, in_sem.at[5]),
        pltpu.make_async_copy(scaling_h, scaling_s, in_sem.at[6]),
        pltpu.make_async_copy(mean_h.at[0], cells.at[0], in_sem.at[0]),
        pltpu.make_async_copy(lon_h.at[0], cells.at[1], in_sem.at[1]),
        pltpu.make_async_copy(lat_h.at[0], cells.at[2], in_sem.at[2]),
    ]
    load_reader = pltpu.make_async_copy(reader_h, reader_s, in_sem.at[7])

    def signal_beside(semaphore):
        for there, step in ((has_south, -1), (has_north, 1)):
            @pl.when(there)
            def _():
                pl.semaphore_signal(semaphore, inc=1, device_id=(band + step, me), device_id_type=MESH)

    def signal_members(semaphore):
        for step in range(1, MEMBERS):
            pl.semaphore_signal(semaphore, inc=1, device_id=(band, (me + step) % MEMBERS), device_id_type=MESH)

    barrier = pltpu.get_barrier_semaphore()
    pl.when(jnp.logical_not(tail_end))(lambda: signal_members(barrier))
    pl.when(jnp.logical_not(answers))(lambda: signal_beside(barrier))
    pl.semaphore_wait(
        barrier,
        jnp.where(tail_end, jnp.where(answers, MEMBERS - 1 + around, MEMBERS - 1), MEMBERS - 2 + around),
    )

    def piece(c, q):
        source = mer_h if c else zon_h
        return source.at[0, q // 2, :, pl.ds(pl.multiple_of((q % 2) * HALF, HALF), HALF)]

    for dy, dx in OFFSETS:
        q = ((chip // 2 + dy) % 4) * 2 + (chip + dx) % 2
        for c in range(2):
            owner = jnp.maximum(2 * q + c, 1)
            spare = (owner != 2 * q + c).astype(jnp.int32)

            def send():
                pltpu.make_async_remote_copy(
                    src_ref=piece(c, q), dst_ref=got.at[spare, me], send_sem=scatter_send,
                    recv_sem=scatter_recv.at[spare], device_id=(band, owner), device_id_type=MESH,
                ).start()

            def keep():
                pltpu.make_async_copy(piece(c, q), got.at[spare, me], own_sem.at[spare]).start()

            if (dy, dx) == (0, 0):
                pl.when(owner != me)(send)
                pl.when(owner == me)(keep)
            else:
                send()

    load_reader.start()
    for load in loads:
        load.start()

    @pl.when(tail_end)
    def _():
        signal_members(late)

    pl.when(answers)(lambda: signal_beside(beside))

    for load in loads[:4]:
        load.wait()
    region = region_v[...]
    weight = jnp.zeros(region.shape, jnp.float32)
    for code in range(REGIONS):
        weight = jnp.where(region == code, scaling_s[0, code], weight)
    land = jnp.where(region < REGIONS // 2, 1.0, 0.4)
    emission = 0.5 * flux_v[...] * land * weight
    zero = jnp.zeros_like(emission)
    below = [zero] + [mix_v[level] for level in range(LEVELS - 1)]
    above = below[1:] + [zero]
    ratios, inverse = [], []
    for level in range(LEVELS):
        denom = 1.0 + below[level] + above[level]
        if level:
            denom = denom + below[level] * ratios[-1]
        inverse.append(1.0 / denom)
        ratios.append(-above[level] * inverse[-1])
    for load in loads[4:]:
        load.wait()
    for k in range(3):
        values = []
        for level in range(LEVELS):
            source = cells[k, level]
            if k == 0 and level == 0:
                source = source + emission
            if level:
                source = source + below[level] * values[-1]
            values.append(source * inverse[level])
        result = values[-1]
        for level in range(LEVELS - 1, -1, -1):
            if level < LEVELS - 1:
                result = values[level] - ratios[level] * result
            cells[k, level] = result
            pack[0, k, pl.ds(2 * level, 2), :] = result[:2]
            pack[1, k, pl.ds(2 * level, 2), :] = result[ROWS - 2:]

    def across(side, part, first, count):
        return pltpu.make_async_remote_copy(
            src_ref=pack.at[side, pl.ds(first, count)], dst_ref=halo.at[1 - side, pl.ds(first, count)],
            send_sem=halo_send.at[part, side], recv_sem=halo_recv.at[part, 1 - side],
            device_id=(band + (1 if side else -1), me), device_id_type=MESH,
        )

    parts = ((0, 3), (U, 1), (V, 1))
    sides = ((0, has_south), (1, has_north))

    def send_across(part):
        for side, there in sides:
            pl.when(there)(across(side, part, *parts[part]).start)

    load_reader.wait()

    @pl.when(jnp.logical_and(tail_end, jnp.logical_not(answers)))
    def _():
        pl.semaphore_wait(beside, around)

    send_across(0)

    most = got.at[0, pl.ds(0, MEMBERS - 1)]

    def arrive(spare):
        kept = got.at[spare, me]
        pltpu.make_async_copy(kept, kept, own_sem.at[spare]).wait()
        pltpu.make_async_copy(most, most, scatter_recv.at[spare]).wait()

    def pass_on(c, q, target):
        pltpu.make_async_remote_copy(
            src_ref=winds.at[c, q], dst_ref=winds.at[c, q], send_sem=gather_send,
            recv_sem=gather_recv.at[c], device_id=(band, target), device_id_type=MESH,
        ).start()

    @pl.when(jnp.logical_not(tail_end))
    def _():
        arrive(0)
        pl.when(me == 1)(lambda: arrive(1))
        winds[core, chip] = got[0, reader_s[0]]
        for dy, dx in OFFSETS:
            q = ((chip // 2 + dy) % 4) * 2 + (chip + dx) % 2
            for c in range(2):
                target = 2 * q + c

                @pl.when(jnp.logical_and(target != me, target != 0))
                def _():
                    pass_on(core, chip, target)

        pl.semaphore_wait(late, 1)
        pass_on(core, chip, 0)

    @pl.when(me == 1)
    def _():
        winds[0, 0] = got[1, reader_s[0]]
        for target in [*range(MEMBERS - 1, 1, -1), 0]:
            pass_on(0, 0, target)

    def await_winds(c):
        mine = jnp.logical_and(jnp.logical_not(tail_end), core == c)
        if c == 0:
            mine = jnp.logical_or(mine, me == 1)
        for count, case in ((CHIPS - 1, mine), (CHIPS, jnp.logical_not(mine))):
            @pl.when(case)
            def _():
                part = winds.at[c, pl.ds(0, count)]
                pltpu.make_async_copy(part, part, gather_recv.at[c]).wait()

    for c in range(2):
        await_winds(c)
        for level in range(LEVELS):
            rows = wind_of(winds, c, level)
            pack[0, U + c, pl.ds(2 * level, 2), :] = rows[:2]
            pack[1, U + c, pl.ds(2 * level, 2), :] = rows[ROWS - 2:]
        send_across(1 + c)

    for level in range(LEVELS):
        new = zonal((cells[0, level], cells[1, level], cells[2, level]), wind_of(winds, 0, level))
        for k in range(3):
            cells[k, level] = new[k]

    for side, there in sides:
        @pl.when(jnp.logical_not(there))
        def _():
            halo[side] = jnp.zeros((5, ROWS, LONS), jnp.float32)

    @pl.when(tail_end)
    def _():
        every = got.at[0]
        pltpu.make_async_copy(every, every, scatter_send).wait()

    @pl.when(jnp.logical_not(tail_end))
    def _():
        sent = got.at[0, pl.ds(0, MEMBERS - 1)]

        @pl.when(me == 1)
        def _():
            some = got.at[0, pl.ds(0, MEMBERS - 2)]
            pltpu.make_async_copy(some, some, scatter_send).wait()
            pltpu.make_async_copy(sent, sent, gather_send).wait()

        @pl.when(me != 1)
        def _():
            pltpu.make_async_copy(sent, sent, scatter_send).wait()

        pltpu.make_async_copy(sent, sent, gather_send).wait()

    for part in range(3):
        for side, there in sides:
            @pl.when(there)
            def _():
                across(side, part, *parts[part]).wait_send()
                across(1 - side, part, *parts[part]).wait_recv()


def finish_kernel(cells_in, winds, halo, out_mean, out_lon, out_lat, cells, edge, south, last, north, out_sem):
    band = lax.axis_index("band")
    bands = lax.axis_size("band")
    first_band, last_band = band == 0, band == bands - 1
    row = lax.broadcasted_iota(jnp.int32, (ROWS, LONS), 0)
    order = (0, 2, 1)
    outs = (out_mean, out_lon, out_lat)

    def up(x):
        return pltpu.roll(x, 1, 0)

    def down(x):
        return pltpu.roll(x, ROWS - 1, 0)

    def meridional(c):
        return (c[0], c[2], c[1])

    s_cells = tuple(halo[0, k] for k in range(3))
    n_cells = tuple(halo[1, k] for k in range(3))
    v_north = jnp.where(last_band, 0.0, halo[1, V])
    for level in range(LEVELS):
        edge[3, pl.ds(2 * level + 1, 1), :] = wind_of(winds, 1, level)[:1]
        edge[3, pl.ds(2 * level, 1), :] = jnp.zeros((1, LONS), jnp.float32)
    stores = []
    for sub in range(SUB):
        source = cells if sub else cells_in
        for level in range(LEVELS):
            here = tuple(source[k, level] for k in range(3))
            if sub:
                here = zonal(here, wind_of(winds, 0, level))
            for k in range(3):
                if sub:
                    cells[k, level] = here[k]
                edge[k, pl.ds(2 * level, 1), :] = here[k][ROWS - 1:]
                edge[k, pl.ds(2 * level + 1, 1), :] = here[k][:1]
        edges = tuple(edge[k] for k in range(3))
        s_cells = tuple(jnp.where(first_band, e, x) for e, x in zip(edges, zonal(s_cells, halo[0, U])))
        n_cells = tuple(jnp.where(last_band, e, x) for e, x in zip(edges, zonal(n_cells, halo[1, U])))
        s_mer, n_mer, e_mer = meridional(s_cells), meridional(n_cells), meridional(edges)
        flux_8 = upwind(v_north, e_mer, n_mer)
        for k in range(3):
            south[k] = s_mer[k]
            last[k] = flux_8[k]
        north[...] = n_cells[0]
        if sub < SUB - 1:
            flux_m1 = upwind(halo[0, V], tuple(up(x) for x in s_mer), s_mer)
            flux_0 = upwind(edge[3], s_mer, e_mer)
            s_cells = meridional(advance(s_mer, flux_m1, flux_0, up(s_mer[0]), e_mer[0]))
            flux_9 = upwind(down(v_north), n_mer, tuple(down(x) for x in n_mer))
            n_cells = meridional(advance(n_mer, flux_8, flux_9, e_mer[0], down(n_mer[0])))
        source = cells if sub else cells_in
        for level in range(LEVELS):
            faces = jnp.where(jnp.logical_and(row == 0, first_band), 0.0, wind_of(winds, 1, level))
            here = tuple(source[k, level] for k in order)
            left = tuple(
                jnp.where(row == 0, south[k, pl.ds(2 * level + 1, 1), :], up(x)) for k, x in enumerate(here)
            )
            flux = upwind(faces, left, here)
            flux_next = tuple(
                jnp.where(row == ROWS - 1, last[k, pl.ds(2 * level, 1), :], down(x)) for k, x in enumerate(flux)
            )
            mean_next = jnp.where(row == ROWS - 1, north[pl.ds(2 * level, 1), :], down(here[0]))
            new = advance(here, flux, flux_next, left[0], mean_next)
            for k, value in zip(order, new):
                cells[k, level] = value
                if sub == SUB - 1:
                    store = pltpu.make_async_copy(cells.at[k, level], outs[k].at[0, level], out_sem.at[k, level])
                    store.start()
                    stores.append(store)
    for store in stores:
        store.wait()


def on_device(*args):
    hbm = pl.BlockSpec(memory_space=pl.ANY)
    local = pl.BlockSpec(memory_space=pltpu.VMEM)
    dma, regular = pltpu.SemaphoreType.DMA, pltpu.SemaphoreType.REGULAR

    def vmem(*dims):
        return pltpu.VMEM(dims, jnp.float32)

    held = pl.pallas_call(
        exchange_kernel,
        out_shape=(vmem(3, LEVELS, ROWS, LONS), vmem(2, CHIPS, ROWS, HALF), vmem(2, 5, ROWS, LONS)),
        in_specs=[hbm] * 10,
        out_specs=(local,) * 3,
        scratch_shapes=[
            vmem(LEVELS - 1, ROWS, LONS),
            vmem(ROWS, LONS),
            pltpu.VMEM((ROWS, LONS), jnp.int32),
            pltpu.SMEM((1, REGIONS), jnp.float32),
            pltpu.SMEM((1,), jnp.int32),
            vmem(2, MEMBERS, ROWS, HALF),
            vmem(2, 5, ROWS, LONS),
            dma((8,)), dma((2,)), dma, dma((2,)), dma, dma((2,)), dma((3, 2)), dma((3, 2)), regular, regular,
        ],
        compiler_params=pltpu.CompilerParams(collective_id=0, has_side_effects=True),
    )(*args)
    held = [pltpu.with_memory_space_constraint(x, pltpu.VMEM) for x in held]
    return pl.pallas_call(
        finish_kernel,
        out_shape=(jax.ShapeDtypeStruct(args[0].shape, jnp.float32),) * 3,
        in_specs=[local] * 3,
        out_specs=(hbm,) * 3,
        scratch_shapes=[
            vmem(3, LEVELS, ROWS, LONS), vmem(4, ROWS, LONS), vmem(3, ROWS, LONS), vmem(3, ROWS, LONS),
            vmem(ROWS, LONS), dma((3, LEVELS)),
        ],
    )(*held)


def solution(mesh):
    moments = P("member", None, "band", None)
    return jax.shard_map(
        on_device,
        mesh=mesh,
        in_specs=(
            moments, moments, moments, moments, moments,
            P(None, "band", None),
            P("band", None),
            P("band", None),
            P("member", None),
            P("band"),
        ),
        out_specs=(moments,) * 3,
        check_vma=False,
    )
```

```python
import jax
import jax.numpy as jnp
from jax import lax
from jax.experimental import pallas as pl
from jax.experimental.pallas import tpu as pltpu
from jax.sharding import PartitionSpec as P

SUB = 2
MESH = pl.DeviceIdType.MESH
LEVELS, ROWS, LONS, REGIONS = 4, 8, 768, 22
MEMBERS, LINE = 16, 8
U, V = 3, 4


def upwind(faces, left, right):
    forward = faces > 0.0
    mean, along, cross = (jnp.where(forward, l, r) for l, r in zip(left, right))
    weight = 0.5 * (jnp.where(forward, 1.0, -1.0) - faces)
    return faces * (mean + weight * along), faces * along, faces * cross


def advance(cells, flux, flux_next, mean_prev, mean_next):
    mean, along, cross = cells
    return (
        mean + (flux[0] - flux_next[0]),
        0.5 * (along + (flux[1] - flux_next[1])) + 0.25 * (mean_next - mean_prev),
        cross + (flux[2] - flux_next[2]),
    )


def zonal(cells, faces):
    count = faces.shape[-1]
    left = tuple(pltpu.roll(x, 1, 1) for x in cells)
    flux = upwind(faces, left, cells)
    flux_next = tuple(pltpu.roll(x, count - 1, 1) for x in flux)
    return advance(cells, flux, flux_next, left[0], pltpu.roll(cells[0], count - 1, 1))


def exchange_kernel(
    mean_h, lon_h, lat_h, zon_h, mer_h, mix_h, flux_h, region_h, scaling_h, reader_h,
    cells, winds, halo,
    mix_v, flux_v, region_v, scaling_s, reader_s, got, tail, mine, theirs, pack,
    in_sem, own_sem, scatter_send, scatter_recv, tail_recv, swap_send, swap_recv, gather_send, gather_recv,
    halo_send, halo_recv, late, beside,
):
    band, me = lax.axis_index("band"), lax.axis_index("member")
    bands = lax.axis_size("band")
    row, line, core = me // 4, (me // 2) % 2, me % 2
    place = 2 * row + core
    has_south, has_north = band > 0, band < bands - 1
    around = has_south.astype(jnp.int32) + has_north.astype(jnp.int32)
    tail_end = me == 0
    answers = jnp.logical_and(tail_end, band % 2 == 0)
    owns = place != 0
    owns_spare = place == 1
    partner = me + 2 - 4 * line

    def member(where, which):
        return (where // 2 * 2 + which) * 2 + where % 2

    loads = [
        pltpu.make_async_copy(mix_h, mix_v, in_sem.at[3]),
        pltpu.make_async_copy(flux_h, flux_v, in_sem.at[4]),
        pltpu.make_async_copy(region_h, region_v, in_sem.at[5]),
        pltpu.make_async_copy(scaling_h, scaling_s, in_sem.at[6]),
        pltpu.make_async_copy(mean_h.at[0], cells.at[0], in_sem.at[0]),
        pltpu.make_async_copy(lon_h.at[0], cells.at[1], in_sem.at[1]),
        pltpu.make_async_copy(lat_h.at[0], cells.at[2], in_sem.at[2]),
    ]
    load_reader = pltpu.make_async_copy(reader_h, reader_s, in_sem.at[7])

    def signal_beside(semaphore):
        for there, step in ((has_south, -1), (has_north, 1)):
            @pl.when(there)
            def _():
                pl.semaphore_signal(semaphore, inc=1, device_id=(band + step, me), device_id_type=MESH)

    def signal_line(semaphore, which, first):
        for step in range(first, LINE):
            target = member((place + step) % LINE, which)
            pl.semaphore_signal(semaphore, inc=1, device_id=(band, target), device_id_type=MESH)

    barrier = pltpu.get_barrier_semaphore()

    @pl.when(jnp.logical_not(tail_end))
    def _():
        signal_line(barrier, line, 1)

        @pl.when(line == 1)
        def _():
            pl.semaphore_signal(barrier, inc=1, device_id=(band, 0), device_id_type=MESH)

        @pl.when(owns)
        def _():
            pl.semaphore_signal(barrier, inc=1, device_id=(band, partner), device_id_type=MESH)

    pl.when(jnp.logical_not(answers))(lambda: signal_beside(barrier))
    others = jnp.where(jnp.logical_and(line == 1, owns), LINE, LINE - 1)
    pl.semaphore_wait(
        barrier,
        jnp.where(tail_end, jnp.where(answers, MEMBERS - 1 + around, MEMBERS - 1), others + around),
    )

    def piece(c, level):
        return (mer_h if c else zon_h).at[0, level]

    def target_of(c, level, which):
        spare = jnp.where(level == 0, 1 - c, 0)
        return spare, member(2 * level + jnp.maximum(c, spare), which)

    @pl.when(tail_end)
    def _():
        for which in (1, 0):
            for level in (2, 1, 3, 0):
                for c in range(2):
                    spare, owner = target_of(c, level, which)
                    pltpu.make_async_remote_copy(
                        src_ref=piece(c, level), dst_ref=tail.at[spare], send_sem=scatter_send,
                        recv_sem=tail_recv.at[spare], device_id=(band, owner), device_id_type=MESH,
                    ).start()
        signal_line(late, 0, 1)

    @pl.when(jnp.logical_not(tail_end))
    def _():
        for step in (2, 1, 3, 0):
            level = (row + step) % LEVELS
            for c in range(2):
                spare, owner = target_of(c, level, line)

                def send():
                    pltpu.make_async_remote_copy(
                        src_ref=piece(c, level), dst_ref=got.at[spare, place], send_sem=scatter_send,
                        recv_sem=scatter_recv.at[spare], device_id=(band, owner), device_id_type=MESH,
                    ).start()

                def keep():
                    pltpu.make_async_copy(piece(c, level), got.at[spare, place], own_sem.at[spare]).start()

                if step:
                    send()
                else:
                    pl.when(owner != me)(send)
                    pl.when(owner == me)(keep)

    load_reader.start()
    for load in loads:
        load.start()

    pl.when(answers)(lambda: signal_beside(beside))

    for load in loads[:4]:
        load.wait()
    region = region_v[...]
    weight = jnp.zeros(region.shape, jnp.float32)
    for code in range(REGIONS):
        weight = jnp.where(region == code, scaling_s[0, code], weight)
    land = jnp.where(region < REGIONS // 2, 1.0, 0.4)
    emission = 0.5 * flux_v[...] * land * weight
    zero = jnp.zeros_like(emission)
    below = [zero] + [mix_v[level] for level in range(LEVELS - 1)]
    above = below[1:] + [zero]
    ratios, inverse = [], []
    for level in range(LEVELS):
        denom = 1.0 + below[level] + above[level]
        if level:
            denom = denom + below[level] * ratios[-1]
        inverse.append(1.0 / denom)
        ratios.append(-above[level] * inverse[-1])
    for load in loads[4:]:
        load.wait()
    for k in range(3):
        values = []
        for level in range(LEVELS):
            source = cells[k, level]
            if k == 0 and level == 0:
                source = source + emission
            if level:
                source = source + below[level] * values[-1]
            values.append(source * inverse[level])
        result = values[-1]
        for level in range(LEVELS - 1, -1, -1):
            if level < LEVELS - 1:
                result = values[level] - ratios[level] * result
            cells[k, level] = result
            pack[0, k, pl.ds(2 * level, 2), :] = result[:2]
            pack[1, k, pl.ds(2 * level, 2), :] = result[ROWS - 2:]

    def across(side, part, first, count):
        return pltpu.make_async_remote_copy(
            src_ref=pack.at[side, pl.ds(first, count)], dst_ref=halo.at[1 - side, pl.ds(first, count)],
            send_sem=halo_send.at[part, side], recv_sem=halo_recv.at[part, 1 - side],
            device_id=(band + (1 if side else -1), me), device_id_type=MESH,
        )

    parts = ((0, 3), (U, 1), (V, 1))
    sides = ((0, has_south), (1, has_north))

    def send_across(part):
        for side, there in sides:
            pl.when(there)(across(side, part, *parts[part]).start)

    load_reader.wait()

    @pl.when(jnp.logical_and(tail_end, jnp.logical_not(answers)))
    def _():
        pl.semaphore_wait(beside, around)

    send_across(0)

    def arrive(spare):
        kept = got.at[spare, place]
        pltpu.make_async_copy(kept, kept, own_sem.at[spare]).wait()
        for count in (LINE - 2, LINE - 1):
            @pl.when(line == count - (LINE - 2))
            def _():
                part = got.at[spare, pl.ds(0, count)]
                pltpu.make_async_copy(part, part, scatter_recv.at[spare]).wait()

    reader = reader_s[0]
    reader_line = (reader // 2) % 2
    reader_place = jnp.maximum(reader // 4 * 2 + reader % 2, 1 - line)

    def swap(spare):
        return pltpu.make_async_remote_copy(
            src_ref=mine.at[spare], dst_ref=theirs.at[spare], send_sem=swap_send.at[spare],
            recv_sem=swap_recv.at[spare], device_id=(band, partner), device_id_type=MESH,
        )

    def offer(spare):
        mine[spare] = got[spare, reader_place]
        swap(spare).start()

    def settle(spare, c, level):
        swap(spare).wait_recv()
        pltpu.make_async_copy(tail.at[spare], tail.at[spare], tail_recv.at[spare]).wait()
        winds[c, level] = jnp.where(
            reader == 0, tail[spare], jnp.where(reader_line == line, mine[spare], theirs[spare])
        )

    def pass_on(c, level, target):
        pltpu.make_async_remote_copy(
            src_ref=winds.at[c, level], dst_ref=winds.at[c, level], send_sem=gather_send,
            recv_sem=gather_recv.at[c], device_id=(band, target), device_id_type=MESH,
        ).start()

    def share(c, level):
        for step in (4, 5, 3, 2, 6, 7, 1):
            target = member((place + step) % LINE, line)
            pl.when(target != 0)(lambda: pass_on(c, level, target))

    @pl.when(owns)
    def _():
        arrive(0)
        pl.when(owns_spare)(lambda: arrive(1))
        offer(0)
        pl.when(owns_spare)(lambda: offer(1))
        settle(0, core, row)
        share(core, row)

        @pl.when(owns_spare)
        def _():
            settle(1, 0, 0)
            share(0, 0)

        @pl.when(line == 0)
        def _():
            pl.semaphore_wait(late, 1)
            pass_on(core, row, 0)
            pl.when(owns_spare)(lambda: pass_on(0, 0, 0))

    def await_winds(c):
        mine_too = jnp.logical_and(owns, jnp.logical_or(core == c, owns_spare))
        for count, case in ((LEVELS - 1, mine_too), (LEVELS, jnp.logical_not(mine_too))):
            @pl.when(case)
            def _():
                part = winds.at[c, pl.ds(0, count)]
                pltpu.make_async_copy(part, part, gather_recv.at[c]).wait()

    for c in range(2):
        await_winds(c)
        for level in range(LEVELS):
            rows = winds[c, level]
            pack[0, U + c, pl.ds(2 * level, 2), :] = rows[:2]
            pack[1, U + c, pl.ds(2 * level, 2), :] = rows[ROWS - 2:]
        send_across(1 + c)

    for level in range(LEVELS):
        new = zonal((cells[0, level], cells[1, level], cells[2, level]), winds[0, level])
        for k in range(3):
            cells[k, level] = new[k]

    for side, there in sides:
        @pl.when(jnp.logical_not(there))
        def _():
            halo[side] = jnp.zeros((5, ROWS, LONS), jnp.float32)

    def drain(count, semaphore):
        part = got.at[0, pl.ds(0, count)]
        pltpu.make_async_copy(part, part, semaphore).wait()

    @pl.when(tail_end)
    def _():
        drain(LINE, scatter_send)
        drain(LINE, scatter_send)

    pl.when(me == 2)(lambda: drain(LINE, scatter_send))

    @pl.when(owns)
    def _():
        drain(LINE - 2, scatter_send)
        swap(0).wait_send()
        drain(LINE - 1, gather_send)

        @pl.when(owns_spare)
        def _():
            swap(1).wait_send()
            drain(LINE - 1, gather_send)

        pl.when(jnp.logical_not(owns_spare))(lambda: drain(1, scatter_send))

    for part in range(3):
        for side, there in sides:
            @pl.when(there)
            def _():
                across(side, part, *parts[part]).wait_send()
                across(1 - side, part, *parts[part]).wait_recv()


def finish_kernel(cells_in, winds, halo, out_mean, out_lon, out_lat, cells, edge, south, last, north, out_sem):
    band = lax.axis_index("band")
    bands = lax.axis_size("band")
    first_band, last_band = band == 0, band == bands - 1
    row = lax.broadcasted_iota(jnp.int32, (ROWS, LONS), 0)
    order = (0, 2, 1)
    outs = (out_mean, out_lon, out_lat)

    def up(x):
        return pltpu.roll(x, 1, 0)

    def down(x):
        return pltpu.roll(x, ROWS - 1, 0)

    def meridional(c):
        return (c[0], c[2], c[1])

    s_cells = tuple(halo[0, k] for k in range(3))
    n_cells = tuple(halo[1, k] for k in range(3))
    v_north = jnp.where(last_band, 0.0, halo[1, V])
    for level in range(LEVELS):
        edge[3, pl.ds(2 * level + 1, 1), :] = winds[1, level][:1]
        edge[3, pl.ds(2 * level, 1), :] = jnp.zeros((1, LONS), jnp.float32)
    stores = []
    for sub in range(SUB):
        source = cells if sub else cells_in
        for level in range(LEVELS):
            here = tuple(source[k, level] for k in range(3))
            if sub:
                here = zonal(here, winds[0, level])
            for k in range(3):
                if sub:
                    cells[k, level] = here[k]
                edge[k, pl.ds(2 * level, 1), :] = here[k][ROWS - 1:]
                edge[k, pl.ds(2 * level + 1, 1), :] = here[k][:1]
        edges = tuple(edge[k] for k in range(3))
        s_cells = tuple(jnp.where(first_band, e, x) for e, x in zip(edges, zonal(s_cells, halo[0, U])))
        n_cells = tuple(jnp.where(last_band, e, x) for e, x in zip(edges, zonal(n_cells, halo[1, U])))
        s_mer, n_mer, e_mer = meridional(s_cells), meridional(n_cells), meridional(edges)
        flux_8 = upwind(v_north, e_mer, n_mer)
        for k in range(3):
            south[k] = s_mer[k]
            last[k] = flux_8[k]
        north[...] = n_cells[0]
        if sub < SUB - 1:
            flux_m1 = upwind(halo[0, V], tuple(up(x) for x in s_mer), s_mer)
            flux_0 = upwind(edge[3], s_mer, e_mer)
            s_cells = meridional(advance(s_mer, flux_m1, flux_0, up(s_mer[0]), e_mer[0]))
            flux_9 = upwind(down(v_north), n_mer, tuple(down(x) for x in n_mer))
            n_cells = meridional(advance(n_mer, flux_8, flux_9, e_mer[0], down(n_mer[0])))
        source = cells if sub else cells_in
        for level in range(LEVELS):
            faces = jnp.where(jnp.logical_and(row == 0, first_band), 0.0, winds[1, level])
            here = tuple(source[k, level] for k in order)
            left = tuple(
                jnp.where(row == 0, south[k, pl.ds(2 * level + 1, 1), :], up(x)) for k, x in enumerate(here)
            )
            flux = upwind(faces, left, here)
            flux_next = tuple(
                jnp.where(row == ROWS - 1, last[k, pl.ds(2 * level, 1), :], down(x)) for k, x in enumerate(flux)
            )
            mean_next = jnp.where(row == ROWS - 1, north[pl.ds(2 * level, 1), :], down(here[0]))
            new = advance(here, flux, flux_next, left[0], mean_next)
            for k, value in zip(order, new):
                cells[k, level] = value
                if sub == SUB - 1:
                    store = pltpu.make_async_copy(cells.at[k, level], outs[k].at[0, level], out_sem.at[k, level])
                    store.start()
                    stores.append(store)
    for store in stores:
        store.wait()


def on_device(*args):
    hbm = pl.BlockSpec(memory_space=pl.ANY)
    local = pl.BlockSpec(memory_space=pltpu.VMEM)
    dma, regular = pltpu.SemaphoreType.DMA, pltpu.SemaphoreType.REGULAR

    def vmem(*dims):
        return pltpu.VMEM(dims, jnp.float32)

    held = pl.pallas_call(
        exchange_kernel,
        out_shape=(vmem(3, LEVELS, ROWS, LONS), vmem(2, LEVELS, ROWS, LONS), vmem(2, 5, ROWS, LONS)),
        in_specs=[hbm] * 10,
        out_specs=(local,) * 3,
        scratch_shapes=[
            vmem(LEVELS - 1, ROWS, LONS),
            vmem(ROWS, LONS),
            pltpu.VMEM((ROWS, LONS), jnp.int32),
            pltpu.SMEM((1, REGIONS), jnp.float32),
            pltpu.SMEM((1,), jnp.int32),
            vmem(2, LINE, ROWS, LONS),
            vmem(2, ROWS, LONS),
            vmem(2, ROWS, LONS),
            vmem(2, ROWS, LONS),
            vmem(2, 5, ROWS, LONS),
            dma((8,)), dma((2,)), dma, dma((2,)), dma((2,)), dma((2,)), dma((2,)), dma, dma((2,)), dma((3, 2)), dma((3, 2)), regular, regular,
        ],
        compiler_params=pltpu.CompilerParams(collective_id=0, has_side_effects=True),
    )(*args)
    held = [pltpu.with_memory_space_constraint(x, pltpu.VMEM) for x in held]
    return pl.pallas_call(
        finish_kernel,
        out_shape=(jax.ShapeDtypeStruct(args[0].shape, jnp.float32),) * 3,
        in_specs=[local] * 3,
        out_specs=(hbm,) * 3,
        scratch_shapes=[
            vmem(3, LEVELS, ROWS, LONS), vmem(4, ROWS, LONS), vmem(3, ROWS, LONS), vmem(3, ROWS, LONS),
            vmem(ROWS, LONS), dma((3, LEVELS)),
        ],
    )(*held)


def solution(mesh):
    moments = P("member", None, "band", None)
    return jax.shard_map(
        on_device,
        mesh=mesh,
        in_specs=(
            moments, moments, moments, moments, moments,
            P(None, "band", None),
            P("band", None),
            P("band", None),
            P("member", None),
            P("band"),
        ),
        out_specs=(moments,) * 3,
        check_vma=False,
    )
```

```python
import jax
import jax.numpy as jnp
from jax import lax
from jax.experimental import pallas as pl
from jax.experimental.pallas import tpu as pltpu
from jax.sharding import PartitionSpec as P

SUB = 2
MESH = pl.DeviceIdType.MESH
LEVELS, ROWS, LONS, REGIONS = 4, 8, 768, 22
LINE = 8
U, V = 3, 4


def upwind(faces, left, right):
    forward = faces > 0.0
    mean, along, cross = (jnp.where(forward, l, r) for l, r in zip(left, right))
    weight = 0.5 * (jnp.where(forward, 1.0, -1.0) - faces)
    return faces * (mean + weight * along), faces * along, faces * cross


def advance(cells, flux, flux_next, mean_prev, mean_next):
    mean, along, cross = cells
    return (
        mean + (flux[0] - flux_next[0]),
        0.5 * (along + (flux[1] - flux_next[1])) + 0.25 * (mean_next - mean_prev),
        cross + (flux[2] - flux_next[2]),
    )


def zonal(cells, faces):
    count = faces.shape[-1]
    left = tuple(pltpu.roll(x, 1, 1) for x in cells)
    flux = upwind(faces, left, cells)
    flux_next = tuple(pltpu.roll(x, count - 1, 1) for x in flux)
    return advance(cells, flux, flux_next, left[0], pltpu.roll(cells[0], count - 1, 1))


def exchange_kernel(
    mean_h, lon_h, lat_h, zon_h, mer_h, mix_h, flux_h, region_h, scaling_h, reader_h,
    cells, winds, halo,
    mix_v, flux_v, region_v, scaling_s, reader_s, got, mine, theirs, slips, slips_in, beyond, pack,
    in_sem, own_sem, scatter_send, scatter_recv, swap_send, swap_recv, slip_send, slip_recv, gather_send, gather_recv,
    halo_send, halo_recv, late, beside,
):
    band, me = lax.axis_index("band"), lax.axis_index("member")
    bands = lax.axis_size("band")
    row, line, core = me // 4, (me // 2) % 2, me % 2
    place = 2 * row + core
    has_south, has_north = band > 0, band < bands - 1
    around = has_south.astype(jnp.int32) + has_north.astype(jnp.int32)
    tail_end = me == 0
    answers = jnp.logical_and(tail_end, band % 2 == 0)
    owns = place != 0
    owns_spare = place == 1
    partner = me + 2 - 4 * line

    def member(where, which):
        return (where // 2 * 2 + which) * 2 + where % 2

    loads = [
        pltpu.make_async_copy(mix_h, mix_v, in_sem.at[3]),
        pltpu.make_async_copy(flux_h, flux_v, in_sem.at[4]),
        pltpu.make_async_copy(region_h, region_v, in_sem.at[5]),
        pltpu.make_async_copy(scaling_h, scaling_s, in_sem.at[6]),
        pltpu.make_async_copy(mean_h.at[0], cells.at[0], in_sem.at[0]),
        pltpu.make_async_copy(lon_h.at[0], cells.at[1], in_sem.at[1]),
        pltpu.make_async_copy(lat_h.at[0], cells.at[2], in_sem.at[2]),
    ]
    load_reader = pltpu.make_async_copy(reader_h, reader_s, in_sem.at[7])

    def signal_beside(semaphore, who):
        for there, step in ((has_south, -1), (has_north, 1)):
            @pl.when(there)
            def _():
                pl.semaphore_signal(semaphore, inc=1, device_id=(band + step, who), device_id_type=MESH)

    def signal_line(semaphore):
        for step in range(1, LINE):
            target = member((place + step) % LINE, line)
            pl.semaphore_signal(semaphore, inc=1, device_id=(band, target), device_id_type=MESH)

    barrier = pltpu.get_barrier_semaphore()

    @pl.when(jnp.logical_not(tail_end))
    def _():
        signal_line(barrier)

    @pl.when(owns)
    def _():
        pl.semaphore_signal(barrier, inc=1, device_id=(band, partner), device_id_type=MESH)
        signal_beside(barrier, partner)

    pl.when(jnp.logical_not(answers))(lambda: signal_beside(barrier, me))
    in_line = jnp.where(jnp.logical_and(line == 0, owns), LINE - 2, LINE - 1)
    outside = jnp.where(owns, 1 + 2 * around, jnp.where(jnp.logical_or(answers, me == 2), around, 0))
    pl.semaphore_wait(barrier, in_line + outside)

    def piece(c, level):
        return (mer_h if c else zon_h).at[0, level]

    def target_of(c, level):
        spare = jnp.where(level == 0, 1 - c, 0)
        return spare, member(2 * level + jnp.maximum(c, spare), line)

    for step in (2, 1, 3, 0):
        level = (row + step) % LEVELS
        for c in range(2):
            spare, owner = target_of(c, level)

            def send():
                pltpu.make_async_remote_copy(
                    src_ref=piece(c, level), dst_ref=got.at[spare, place], send_sem=scatter_send,
                    recv_sem=scatter_recv.at[spare], device_id=(band, owner), device_id_type=MESH,
                ).start()

            def keep():
                pltpu.make_async_copy(piece(c, level), got.at[spare, place], own_sem.at[spare]).start()

            if step:
                send()
            else:
                pl.when(owner != me)(send)
                pl.when(owner == me)(keep)

    pl.when(tail_end)(lambda: signal_line(late))

    load_reader.start()
    for load in loads:
        load.start()

    pl.when(answers)(lambda: signal_beside(beside, me))

    for load in loads[:4]:
        load.wait()
    region = region_v[...]
    weight = jnp.zeros(region.shape, jnp.float32)
    for code in range(REGIONS):
        weight = jnp.where(region == code, scaling_s[0, code], weight)
    land = jnp.where(region < REGIONS // 2, 1.0, 0.4)
    emission = 0.5 * flux_v[...] * land * weight
    zero = jnp.zeros_like(emission)
    below = [zero] + [mix_v[level] for level in range(LEVELS - 1)]
    above = below[1:] + [zero]
    ratios, inverse = [], []
    for level in range(LEVELS):
        denom = 1.0 + below[level] + above[level]
        if level:
            denom = denom + below[level] * ratios[-1]
        inverse.append(1.0 / denom)
        ratios.append(-above[level] * inverse[-1])
    for load in loads[4:]:
        load.wait()
    for k in range(3):
        values = []
        for level in range(LEVELS):
            source = cells[k, level]
            if k == 0 and level == 0:
                source = source + emission
            if level:
                source = source + below[level] * values[-1]
            values.append(source * inverse[level])
        result = values[-1]
        for level in range(LEVELS - 1, -1, -1):
            if level < LEVELS - 1:
                result = values[level] - ratios[level] * result
            cells[k, level] = result
            pack[0, k, pl.ds(2 * level, 2), :] = result[:2]
            pack[1, k, pl.ds(2 * level, 2), :] = result[ROWS - 2:]

    def across(side):
        return pltpu.make_async_remote_copy(
            src_ref=pack.at[side], dst_ref=halo.at[1 - side, pl.ds(0, 3)],
            send_sem=halo_send.at[side], recv_sem=halo_recv.at[1 - side],
            device_id=(band + (1 if side else -1), me), device_id_type=MESH,
        )

    sides = ((0, has_south), (1, has_north))

    load_reader.wait()

    @pl.when(jnp.logical_and(tail_end, jnp.logical_not(answers)))
    def _():
        pl.semaphore_wait(beside, around)

    for side, there in sides:
        pl.when(there)(across(side).start)

    def arrive(spare):
        kept = got.at[spare, place]
        pltpu.make_async_copy(kept, kept, own_sem.at[spare]).wait()
        part = got.at[spare, pl.ds(0, LINE - 1)]
        pltpu.make_async_copy(part, part, scatter_recv.at[spare]).wait()

    reader = reader_s[0]
    here = (reader // 2) % 2 == line
    reader_place = reader // 4 * 2 + reader % 2

    def swap(spare):
        return pltpu.make_async_remote_copy(
            src_ref=mine.at[spare], dst_ref=theirs.at[spare], send_sem=swap_send.at[spare],
            recv_sem=swap_recv.at[spare], device_id=(band, partner), device_id_type=MESH,
        )

    def slip(spare, side, other):
        return pltpu.make_async_remote_copy(
            src_ref=slips.at[spare, side], dst_ref=slips_in.at[spare, 1 - side, other],
            send_sem=slip_send.at[spare, side, other], recv_sem=slip_recv.at[spare, 1 - side, other],
            device_id=(band + (1 if side else -1), partner if other else me), device_id_type=MESH,
        )

    def offer(spare):
        chosen = got[spare, reader_place]
        mine[spare] = chosen
        swap(spare).start()
        slips[spare, 0] = jnp.where(here, chosen[:2], 0.0)
        slips[spare, 1] = jnp.where(here, chosen[ROWS - 2:], 0.0)
        for side, there in sides:
            for other in (1, 0):
                pl.when(there)(slip(spare, side, other).start)

    def settle(spare, c, level):
        swap(spare).wait_recv()
        winds[c, level] = jnp.where(here, mine[spare], theirs[spare])

    def settle_beside(spare, c, level):
        for side, there in sides:
            @pl.when(there)
            def _():
                for other in range(2):
                    slip(spare, 1 - side, other).wait_recv()
                beyond[c, level, pl.ds(2 * side, 2), :] = slips_in[spare, side, 0] + slips_in[spare, side, 1]

            @pl.when(jnp.logical_not(there))
            def _():
                beyond[c, level, pl.ds(2 * side, 2), :] = jnp.zeros((2, LONS), jnp.float32)

    def pass_on(ref, part, c, level, target):
        pltpu.make_async_remote_copy(
            src_ref=ref.at[c, level], dst_ref=ref.at[c, level], send_sem=gather_send.at[part],
            recv_sem=gather_recv.at[part, c], device_id=(band, target), device_id_type=MESH,
        ).start()

    def share(ref, part, c, level):
        for step in (4, 5, 3, 2, 6, 7, 1):
            target = member((place + step) % LINE, line)
            pl.when(target != 0)(lambda: pass_on(ref, part, c, level, target))

    @pl.when(owns)
    def _():
        arrive(0)
        pl.when(owns_spare)(lambda: arrive(1))
        offer(0)
        pl.when(owns_spare)(lambda: offer(1))
        settle(0, core, row)
        share(winds, 0, core, row)

        @pl.when(owns_spare)
        def _():
            settle(1, 0, 0)
            share(winds, 0, 0, 0)

        settle_beside(0, core, row)
        share(beyond, 1, core, row)

        @pl.when(owns_spare)
        def _():
            settle_beside(1, 0, 0)
            share(beyond, 1, 0, 0)

        @pl.when(line == 0)
        def _():
            pl.semaphore_wait(late, 1)
            for part, ref in enumerate((winds, beyond)):
                pass_on(ref, part, core, row, 0)
                pl.when(owns_spare)(lambda: pass_on(ref, part, 0, 0, 0))

    def await_winds(ref, part, c):
        mine_too = jnp.logical_and(owns, jnp.logical_or(core == c, owns_spare))
        for count, case in ((LEVELS - 1, mine_too), (LEVELS, jnp.logical_not(mine_too))):
            @pl.when(case)
            def _():
                some = ref.at[c, pl.ds(0, count)]
                pltpu.make_async_copy(some, some, gather_recv.at[part, c]).wait()

    await_winds(winds, 0, 0)
    for level in range(LEVELS):
        new = zonal((cells[0, level], cells[1, level], cells[2, level]), winds[0, level])
        for k in range(3):
            cells[k, level] = new[k]

    await_winds(winds, 0, 1)
    for c in range(2):
        await_winds(beyond, 1, c)
        for level in range(LEVELS):
            for side in range(2):
                halo[side, U + c, pl.ds(2 * level, 2), :] = beyond[c, level, pl.ds(2 * side, 2), :]

    def drain(ref, count, semaphore):
        some = ref.at[0, pl.ds(0, count)]
        pltpu.make_async_copy(some, some, semaphore).wait()

    def drain_owner(spare):
        swap(spare).wait_send()
        for side, there in sides:
            for other in range(2):
                pl.when(there)(slip(spare, side, other).wait_send)
        for part, ref in enumerate((winds, beyond)):
            drain(ref, LEVELS, gather_send.at[part])
            drain(ref, LEVELS - 1, gather_send.at[part])

    drain(got, LINE - 2, scatter_send)
    pl.when(jnp.logical_not(owns))(lambda: drain(got, 2, scatter_send))

    @pl.when(owns)
    def _():
        drain_owner(0)
        pl.when(owns_spare)(lambda: drain_owner(1))
        pl.when(jnp.logical_not(owns_spare))(lambda: drain(got, 1, scatter_send))

    for side, there in sides:
        @pl.when(there)
        def _():
            across(side).wait_send()
            across(1 - side).wait_recv()

        @pl.when(jnp.logical_not(there))
        def _():
            halo[side, pl.ds(0, 3)] = jnp.zeros((3, ROWS, LONS), jnp.float32)


def finish_kernel(cells_in, winds, halo, out_mean, out_lon, out_lat, cells, edge, south, last, north, out_sem):
    band = lax.axis_index("band")
    bands = lax.axis_size("band")
    first_band, last_band = band == 0, band == bands - 1
    row = lax.broadcasted_iota(jnp.int32, (ROWS, LONS), 0)
    order = (0, 2, 1)
    outs = (out_mean, out_lon, out_lat)

    def up(x):
        return pltpu.roll(x, 1, 0)

    def down(x):
        return pltpu.roll(x, ROWS - 1, 0)

    def meridional(c):
        return (c[0], c[2], c[1])

    s_cells = tuple(halo[0, k] for k in range(3))
    n_cells = tuple(halo[1, k] for k in range(3))
    v_north = jnp.where(last_band, 0.0, halo[1, V])
    for level in range(LEVELS):
        edge[3, pl.ds(2 * level + 1, 1), :] = winds[1, level][:1]
        edge[3, pl.ds(2 * level, 1), :] = jnp.zeros((1, LONS), jnp.float32)
    stores = []
    for sub in range(SUB):
        source = cells if sub else cells_in
        for level in range(LEVELS):
            here = tuple(source[k, level] for k in range(3))
            if sub:
                here = zonal(here, winds[0, level])
            for k in range(3):
                if sub:
                    cells[k, level] = here[k]
                edge[k, pl.ds(2 * level, 1), :] = here[k][ROWS - 1:]
                edge[k, pl.ds(2 * level + 1, 1), :] = here[k][:1]
        edges = tuple(edge[k] for k in range(3))
        s_cells = tuple(jnp.where(first_band, e, x) for e, x in zip(edges, zonal(s_cells, halo[0, U])))
        n_cells = tuple(jnp.where(last_band, e, x) for e, x in zip(edges, zonal(n_cells, halo[1, U])))
        s_mer, n_mer, e_mer = meridional(s_cells), meridional(n_cells), meridional(edges)
        flux_8 = upwind(v_north, e_mer, n_mer)
        for k in range(3):
            south[k] = s_mer[k]
            last[k] = flux_8[k]
        north[...] = n_cells[0]
        if sub < SUB - 1:
            flux_m1 = upwind(halo[0, V], tuple(up(x) for x in s_mer), s_mer)
            flux_0 = upwind(edge[3], s_mer, e_mer)
            s_cells = meridional(advance(s_mer, flux_m1, flux_0, up(s_mer[0]), e_mer[0]))
            flux_9 = upwind(down(v_north), n_mer, tuple(down(x) for x in n_mer))
            n_cells = meridional(advance(n_mer, flux_8, flux_9, e_mer[0], down(n_mer[0])))
        source = cells if sub else cells_in
        for level in range(LEVELS):
            faces = jnp.where(jnp.logical_and(row == 0, first_band), 0.0, winds[1, level])
            here = tuple(source[k, level] for k in order)
            left = tuple(
                jnp.where(row == 0, south[k, pl.ds(2 * level + 1, 1), :], up(x)) for k, x in enumerate(here)
            )
            flux = upwind(faces, left, here)
            flux_next = tuple(
                jnp.where(row == ROWS - 1, last[k, pl.ds(2 * level, 1), :], down(x)) for k, x in enumerate(flux)
            )
            mean_next = jnp.where(row == ROWS - 1, north[pl.ds(2 * level, 1), :], down(here[0]))
            new = advance(here, flux, flux_next, left[0], mean_next)
            for k, value in zip(order, new):
                cells[k, level] = value
                if sub == SUB - 1:
                    store = pltpu.make_async_copy(cells.at[k, level], outs[k].at[0, level], out_sem.at[k, level])
                    store.start()
                    stores.append(store)
    for store in stores:
        store.wait()


def on_device(*args):
    hbm = pl.BlockSpec(memory_space=pl.ANY)
    local = pl.BlockSpec(memory_space=pltpu.VMEM)
    dma, regular = pltpu.SemaphoreType.DMA, pltpu.SemaphoreType.REGULAR

    def vmem(*dims):
        return pltpu.VMEM(dims, jnp.float32)

    held = pl.pallas_call(
        exchange_kernel,
        out_shape=(vmem(3, LEVELS, ROWS, LONS), vmem(2, LEVELS, ROWS, LONS), vmem(2, 5, ROWS, LONS)),
        in_specs=[hbm] * 10,
        out_specs=(local,) * 3,
        scratch_shapes=[
            vmem(LEVELS - 1, ROWS, LONS),
            vmem(ROWS, LONS),
            pltpu.VMEM((ROWS, LONS), jnp.int32),
            pltpu.SMEM((1, REGIONS), jnp.float32),
            pltpu.SMEM((1,), jnp.int32),
            vmem(2, LINE, ROWS, LONS),
            vmem(2, ROWS, LONS),
            vmem(2, ROWS, LONS),
            vmem(2, 2, 2, LONS),
            vmem(2, 2, 2, 2, LONS),
            vmem(2, LEVELS, 4, LONS),
            vmem(2, 3, ROWS, LONS),
            dma((8,)), dma((2,)), dma, dma((2,)), dma((2,)), dma((2,)), dma((2, 2, 2)), dma((2, 2, 2)), dma((2,)), dma((2, 2)),
            dma((2,)), dma((2,)), regular, regular,
        ],
        compiler_params=pltpu.CompilerParams(collective_id=0, has_side_effects=True),
    )(*args)
    held = [pltpu.with_memory_space_constraint(x, pltpu.VMEM) for x in held]
    return pl.pallas_call(
        finish_kernel,
        out_shape=(jax.ShapeDtypeStruct(args[0].shape, jnp.float32),) * 3,
        in_specs=[local] * 3,
        out_specs=(hbm,) * 3,
        scratch_shapes=[
            vmem(3, LEVELS, ROWS, LONS), vmem(4, ROWS, LONS), vmem(3, ROWS, LONS), vmem(3, ROWS, LONS),
            vmem(ROWS, LONS), dma((3, LEVELS)),
        ],
    )(*held)


def solution(mesh):
    moments = P("member", None, "band", None)
    return jax.shard_map(
        on_device,
        mesh=mesh,
        in_specs=(
            moments, moments, moments, moments, moments,
            P(None, "band", None),
            P("band", None),
            P("band", None),
            P("member", None),
            P("band"),
        ),
        out_specs=(moments,) * 3,
        check_vma=False,
    )
```

```python
import jax
import jax.numpy as jnp
from jax import lax
from jax.experimental import pallas as pl
from jax.experimental.pallas import tpu as pltpu
from jax.sharding import PartitionSpec as P

SUB = 2
MESH = pl.DeviceIdType.MESH
LEVELS, ROWS, LONS, REGIONS = 4, 8, 768, 22
LINE, HALF = 8, 384


def upwind(faces, left, right):
    forward = faces > 0.0
    mean, along, cross = (jnp.where(forward, l, r) for l, r in zip(left, right))
    weight = 0.5 * (jnp.where(forward, 1.0, -1.0) - faces)
    return faces * (mean + weight * along), faces * along, faces * cross


def advance(cells, flux, flux_next, mean_prev, mean_next):
    mean, along, cross = cells
    return (
        mean + (flux[0] - flux_next[0]),
        0.5 * (along + (flux[1] - flux_next[1])) + 0.25 * (mean_next - mean_prev),
        cross + (flux[2] - flux_next[2]),
    )


def zonal(cells, faces):
    count = faces.shape[-1]
    left = tuple(pltpu.roll(x, 1, 1) for x in cells)
    flux = upwind(faces, left, cells)
    flux_next = tuple(pltpu.roll(x, count - 1, 1) for x in flux)
    return advance(cells, flux, flux_next, left[0], pltpu.roll(cells[0], count - 1, 1))


def wind_of(winds, c, level):
    return jnp.concatenate([winds[c, 2 * level], winds[c, 2 * level + 1]], -1)


def step_kernel(
    mean_h, lon_h, lat_h, zon_h, mer_h, mix_h, flux_h, region_h, scaling_h, reader_h,
    cells,
    mix_v, flux_v, region_v, scaling_s, reader_s, got_u, got_v, got_spare_u, got_spare_v, mine, theirs, slips, slips_in,
    winds, beyond, pack, halo, edge, south, last, north,
    in_sem, own_sem, scatter_send, scatter_recv, swap_send, swap_recv, slip_send, slip_recv, gather_send, gather_recv,
    halo_send, halo_recv, late, beside,
):
    band, me = lax.axis_index("band"), lax.axis_index("member")
    bands = lax.axis_size("band")
    line = (me // 2) % 2
    place = me // 4 * 2 + me % 2
    got = ((got_u, got_v), (got_spare_u, got_spare_v))
    has_south, has_north = band > 0, band < bands - 1
    around = has_south.astype(jnp.int32) + has_north.astype(jnp.int32)
    tail_end = me == 0
    answers = jnp.logical_and(tail_end, band % 2 == 0)
    owns = place != 0
    owns_spare = place == 1
    partner = me + 2 - 4 * line

    def member(where, which):
        return (where // 2 * 2 + which) * 2 + where % 2

    loads = [
        pltpu.make_async_copy(mix_h, mix_v, in_sem.at[3]),
        pltpu.make_async_copy(flux_h, flux_v, in_sem.at[4]),
        pltpu.make_async_copy(region_h, region_v, in_sem.at[5]),
        pltpu.make_async_copy(scaling_h, scaling_s, in_sem.at[6]),
        pltpu.make_async_copy(mean_h.at[0], cells.at[0], in_sem.at[0]),
        pltpu.make_async_copy(lon_h.at[0], cells.at[1], in_sem.at[1]),
        pltpu.make_async_copy(lat_h.at[0], cells.at[2], in_sem.at[2]),
    ]
    load_reader = pltpu.make_async_copy(reader_h, reader_s, in_sem.at[7])

    def signal_beside(semaphore, who):
        for there, step in ((has_south, -1), (has_north, 1)):
            @pl.when(there)
            def _():
                pl.semaphore_signal(semaphore, inc=1, device_id=(band + step, who), device_id_type=MESH)

    def signal_line(semaphore):
        for step in range(1, LINE):
            target = member((place + step) % LINE, line)
            pl.semaphore_signal(semaphore, inc=1, device_id=(band, target), device_id_type=MESH)

    barrier = pltpu.get_barrier_semaphore()

    @pl.when(jnp.logical_not(tail_end))
    def _():
        signal_line(barrier)

    @pl.when(owns)
    def _():
        pl.semaphore_signal(barrier, inc=1, device_id=(band, partner), device_id_type=MESH)
        signal_beside(barrier, partner)

    pl.when(jnp.logical_not(answers))(lambda: signal_beside(barrier, me))
    in_line = jnp.where(jnp.logical_and(line == 0, owns), LINE - 2, LINE - 1)
    outside = jnp.where(owns, 1 + 2 * around, jnp.where(jnp.logical_or(answers, me == 2), around, 0))
    pl.semaphore_wait(barrier, in_line + outside)

    def piece(c, there):
        return (mer_h if c else zon_h).at[0, there // 2, :, pl.ds(pl.multiple_of(there % 2 * HALF, HALF), HALF)]

    for c in range(2):
        for step in (4, 5, 3, 2, 6, 7, 1, 0):
            there = (place + step) % LINE
            for spare in range(2):
                def send():
                    pltpu.make_async_remote_copy(
                        src_ref=piece(c, there), dst_ref=got[spare][c].at[place], send_sem=scatter_send,
                        recv_sem=scatter_recv.at[spare, c], device_id=(band, member(jnp.maximum(there, 1), line)),
                        device_id_type=MESH,
                    ).start()

                def keep():
                    pltpu.make_async_copy(piece(c, there), got[spare][c].at[place], own_sem.at[spare, c]).start()

                fits = there == 0 if spare else there != 0
                if step in (0, 7):
                    pl.when(jnp.logical_and(fits, jnp.maximum(there, 1) == place))(keep)
                    pl.when(jnp.logical_and(fits, jnp.maximum(there, 1) != place))(send)
                else:
                    pl.when(fits)(send)

    pl.when(tail_end)(lambda: signal_line(late))

    load_reader.start()
    for load in loads:
        load.start()

    pl.when(answers)(lambda: signal_beside(beside, me))

    for load in loads[:4]:
        load.wait()
    region = region_v[...]
    weight = jnp.zeros(region.shape, jnp.float32)
    for code in range(REGIONS):
        weight = jnp.where(region == code, scaling_s[0, code], weight)
    land = jnp.where(region < REGIONS // 2, 1.0, 0.4)
    emission = 0.5 * flux_v[...] * land * weight
    zero = jnp.zeros_like(emission)
    below = [zero] + [mix_v[level] for level in range(LEVELS - 1)]
    above = below[1:] + [zero]
    ratios, inverse = [], []
    for level in range(LEVELS):
        denom = 1.0 + below[level] + above[level]
        if level:
            denom = denom + below[level] * ratios[-1]
        inverse.append(1.0 / denom)
        ratios.append(-above[level] * inverse[-1])
    for load in loads[4:]:
        load.wait()
    for k in range(3):
        values = []
        for level in range(LEVELS):
            source = cells[k, level]
            if k == 0 and level == 0:
                source = source + emission
            if level:
                source = source + below[level] * values[-1]
            values.append(source * inverse[level])
        result = values[-1]
        for level in range(LEVELS - 1, -1, -1):
            if level < LEVELS - 1:
                result = values[level] - ratios[level] * result
            cells[k, level] = result
            pack[0, k, pl.ds(2 * level, 2), :] = result[:2]
            pack[1, k, pl.ds(2 * level, 2), :] = result[ROWS - 2:]

    def across(side):
        return pltpu.make_async_remote_copy(
            src_ref=pack.at[side], dst_ref=halo.at[1 - side, pl.ds(0, 3)],
            send_sem=halo_send.at[side], recv_sem=halo_recv.at[1 - side],
            device_id=(band + (1 if side else -1), me), device_id_type=MESH,
        )

    sides = ((0, has_south), (1, has_north))

    load_reader.wait()

    @pl.when(jnp.logical_and(tail_end, jnp.logical_not(answers)))
    def _():
        pl.semaphore_wait(beside, around)

    for side, there in sides:
        pl.when(there)(across(side).start)

    def arrive(spare, c):
        kept = got[spare][c].at[place]
        pltpu.make_async_copy(kept, kept, own_sem.at[spare, c]).wait()
        part = got[spare][c].at[pl.ds(0, LINE - 1)]
        pltpu.make_async_copy(part, part, scatter_recv.at[spare, c]).wait()

    reader = reader_s[0]
    here = (reader // 2) % 2 == line
    reader_place = reader // 4 * 2 + reader % 2

    def swap(spare, c):
        return pltpu.make_async_remote_copy(
            src_ref=mine.at[spare, c], dst_ref=theirs.at[spare, c], send_sem=swap_send.at[spare, c],
            recv_sem=swap_recv.at[spare, c], device_id=(band, partner), device_id_type=MESH,
        )

    def slip(spare, c, side, other):
        return pltpu.make_async_remote_copy(
            src_ref=slips.at[spare, c, side], dst_ref=slips_in.at[spare, c, 1 - side, other],
            send_sem=slip_send.at[spare, c, side, other], recv_sem=slip_recv.at[spare, c, 1 - side, other],
            device_id=(band + (1 if side else -1), partner if other else me), device_id_type=MESH,
        )

    def offer(spare, c):
        chosen = got[spare][c][reader_place]
        mine[spare, c] = chosen
        swap(spare, c).start()
        slips[spare, c, 0] = jnp.where(here, chosen[:2], 0.0)
        slips[spare, c, 1] = jnp.where(here, chosen[ROWS - 2:], 0.0)
        for side, there in sides:
            for other in (1, 0):
                pl.when(there)(slip(spare, c, side, other).start)

    def share(ref, part, c, whose):
        for step in (4, 5, 3, 2, 6, 7, 1):
            target = member((place + step) % LINE, line)
            pltpu.make_async_remote_copy(
                src_ref=ref.at[c, whose], dst_ref=ref.at[c, whose], send_sem=gather_send.at[part, c],
                recv_sem=gather_recv.at[part, c], device_id=(band, target), device_id_type=MESH,
            ).start()

    def settle(spare, c):
        swap(spare, c).wait_recv()
        whose = 0 if spare else place
        winds[c, whose] = jnp.where(here, mine[spare, c], theirs[spare, c])
        share(winds, 0, c, whose)

    def settle_beside(spare, c):
        whose = 0 if spare else place
        for side, there in sides:
            @pl.when(there)
            def _():
                for other in range(2):
                    slip(spare, c, 1 - side, other).wait_recv()
                both = slips_in[spare, c, side, 0] + slips_in[spare, c, side, 1]
                beyond[c, whose, pl.ds(2 * side, 2), :] = both

            @pl.when(jnp.logical_not(there))
            def _():
                beyond[c, whose, pl.ds(2 * side, 2), :] = jnp.zeros((2, HALF), jnp.float32)

        share(beyond, 1, c, whose)

    @pl.when(owns)
    def _():
        for c in range(2):
            arrive(0, c)
            offer(0, c)

            @pl.when(owns_spare)
            def _():
                arrive(1, c)
                offer(1, c)

        @pl.when(line == 0)
        def _():
            pl.semaphore_wait(late, 1)

        for c in range(2):
            settle(0, c)
            pl.when(owns_spare)(lambda: settle(1, c))
            settle_beside(0, c)
            pl.when(owns_spare)(lambda: settle_beside(1, c))

    def await_winds(ref, part, c):
        cases = ((0, jnp.logical_not(owns)), (1, jnp.logical_and(owns, jnp.logical_not(owns_spare))), (2, owns_spare))
        for owned, case in cases:
            @pl.when(case)
            def _():
                some = ref.at[c, pl.ds(0, LINE - owned)]
                pltpu.make_async_copy(some, some, gather_recv.at[part, c]).wait()

    def halo_wind(c):
        await_winds(beyond, 1, c)
        for there in range(LINE):
            for side in range(2):
                place_rows = (pl.ds(there // 2 * 2, 2), pl.ds(there % 2 * HALF, HALF))
                halo[side, 3 + c, *place_rows] = beyond[c, there, pl.ds(2 * side, 2), :]

    row = lax.broadcasted_iota(jnp.int32, (ROWS, LONS), 0)
    order = (0, 2, 1)

    def up(x):
        return pltpu.roll(x, 1, 0)

    def down(x):
        return pltpu.roll(x, ROWS - 1, 0)

    def meridional(c):
        return (c[0], c[2], c[1])

    no_south, no_north = jnp.logical_not(has_south), jnp.logical_not(has_north)
    for sub in range(SUB):
        if sub == 0:
            await_winds(winds, 0, 0)
        for level in range(LEVELS):
            swept = zonal(tuple(cells[k, level] for k in range(3)), wind_of(winds, 0, level))
            for k in range(3):
                cells[k, level] = swept[k]
                edge[k, pl.ds(2 * level, 1), :] = swept[k][ROWS - 1:]
                edge[k, pl.ds(2 * level + 1, 1), :] = swept[k][:1]
        if sub == 0:
            for side, there in sides:
                @pl.when(there)
                def _():
                    across(1 - side).wait_recv()

                @pl.when(jnp.logical_not(there))
                def _():
                    halo[side, pl.ds(0, 3)] = jnp.zeros((3, ROWS, LONS), jnp.float32)

            halo_wind(0)
            s_cells = tuple(halo[0, k] for k in range(3))
            n_cells = tuple(halo[1, k] for k in range(3))
        edges = tuple(edge[k] for k in range(3))
        s_cells = tuple(jnp.where(no_south, e, x) for e, x in zip(edges, zonal(s_cells, halo[0, 3])))
        n_cells = tuple(jnp.where(no_north, e, x) for e, x in zip(edges, zonal(n_cells, halo[1, 3])))
        s_mer, n_mer, e_mer = meridional(s_cells), meridional(n_cells), meridional(edges)
        if sub == 0:
            await_winds(winds, 0, 1)
            halo_wind(1)
            v_north = jnp.where(no_north, 0.0, halo[1, 4])
            for level in range(LEVELS):
                edge[3, pl.ds(2 * level + 1, 1), :] = wind_of(winds, 1, level)[:1]
                edge[3, pl.ds(2 * level, 1), :] = jnp.zeros((1, LONS), jnp.float32)
        flux_8 = upwind(v_north, e_mer, n_mer)
        for k in range(3):
            south[k] = s_mer[k]
            last[k] = flux_8[k]
        north[...] = n_cells[0]
        if sub < SUB - 1:
            flux_m1 = upwind(halo[0, 4], tuple(up(x) for x in s_mer), s_mer)
            flux_0 = upwind(edge[3], s_mer, e_mer)
            s_cells = meridional(advance(s_mer, flux_m1, flux_0, up(s_mer[0]), e_mer[0]))
            flux_9 = upwind(down(v_north), n_mer, tuple(down(x) for x in n_mer))
            n_cells = meridional(advance(n_mer, flux_8, flux_9, e_mer[0], down(n_mer[0])))
        for level in range(LEVELS):
            faces = jnp.where(jnp.logical_and(row == 0, no_south), 0.0, wind_of(winds, 1, level))
            now = tuple(cells[k, level] for k in order)
            left = tuple(
                jnp.where(row == 0, south[k, pl.ds(2 * level + 1, 1), :], up(x)) for k, x in enumerate(now)
            )
            flux = upwind(faces, left, now)
            flux_next = tuple(
                jnp.where(row == ROWS - 1, last[k, pl.ds(2 * level, 1), :], down(x)) for k, x in enumerate(flux)
            )
            mean_next = jnp.where(row == ROWS - 1, north[pl.ds(2 * level, 1), :], down(now[0]))
            new = advance(now, flux, flux_next, left[0], mean_next)
            for k, value in zip(order, new):
                cells[k, level] = value

    def drain(ref, count, semaphore):
        some = ref.at[pl.ds(0, count)]
        pltpu.make_async_copy(some, some, semaphore).wait()

    def drain_owner(spare, c):
        swap(spare, c).wait_send()
        for side, there in sides:
            for other in range(2):
                pl.when(there)(slip(spare, c, side, other).wait_send)
        for part, ref in enumerate((winds, beyond)):
            drain(ref.at[c], LINE - 1, gather_send.at[part, c])

    for c in range(2):
        drain(got_u, LINE - 2, scatter_send)
        pl.when(jnp.logical_not(owns))(lambda: drain(got_u, 2, scatter_send))

        @pl.when(owns)
        def _():
            drain_owner(0, c)
            pl.when(owns_spare)(lambda: drain_owner(1, c))
            pl.when(jnp.logical_not(owns_spare))(lambda: drain(got_u, 1, scatter_send))

    for side, there in sides:
        pl.when(there)(across(side).wait_send)


def store_kernel(cells, out_mean, out_lon, out_lat, out_sem):
    stores = [
        pltpu.make_async_copy(cells.at[k], out.at[0], out_sem.at[k]) for k, out in enumerate((out_mean, out_lon, out_lat))
    ]
    for store in stores:
        store.start()
    for store in stores:
        store.wait()


def on_device(*args):
    hbm = pl.BlockSpec(memory_space=pl.ANY)
    local = pl.BlockSpec(memory_space=pltpu.VMEM)
    dma, regular = pltpu.SemaphoreType.DMA, pltpu.SemaphoreType.REGULAR

    def vmem(*dims):
        return pltpu.VMEM(dims, jnp.float32)

    cells = pl.pallas_call(
        step_kernel,
        out_shape=vmem(3, LEVELS, ROWS, LONS),
        in_specs=[hbm] * 10,
        out_specs=local,
        scratch_shapes=[
            vmem(LEVELS - 1, ROWS, LONS),
            vmem(ROWS, LONS),
            pltpu.VMEM((ROWS, LONS), jnp.int32),
            pltpu.SMEM((1, REGIONS), jnp.float32),
            pltpu.SMEM((1,), jnp.int32),
            *[vmem(LINE, ROWS, HALF)] * 4,
            vmem(2, 2, ROWS, HALF),
            vmem(2, 2, ROWS, HALF),
            vmem(2, 2, 2, 2, HALF),
            vmem(2, 2, 2, 2, 2, HALF),
            vmem(2, LINE, ROWS, HALF),
            vmem(2, LINE, 4, HALF),
            vmem(2, 3, ROWS, LONS),
            vmem(2, 5, ROWS, LONS),
            vmem(4, ROWS, LONS),
            vmem(3, ROWS, LONS),
            vmem(3, ROWS, LONS),
            vmem(ROWS, LONS),
            dma((8,)), dma((2, 2)), dma, dma((2, 2)), dma((2, 2)), dma((2, 2)), dma((2, 2, 2, 2)), dma((2, 2, 2, 2)),
            dma((2, 2)), dma((2, 2)), dma((2,)), dma((2,)), regular, regular,
        ],
        compiler_params=pltpu.CompilerParams(collective_id=0, has_side_effects=True),
    )(*args)
    return pl.pallas_call(
        store_kernel,
        out_shape=(jax.ShapeDtypeStruct(args[0].shape, jnp.float32),) * 3,
        in_specs=[local],
        out_specs=(hbm,) * 3,
        scratch_shapes=[dma((3,))],
    )(pltpu.with_memory_space_constraint(cells, pltpu.VMEM))


def solution(mesh):
    moments = P("member", None, "band", None)
    return jax.shard_map(
        on_device,
        mesh=mesh,
        in_specs=(
            moments, moments, moments, moments, moments,
            P(None, "band", None),
            P("band", None),
            P("band", None),
            P("member", None),
            P("band"),
        ),
        out_specs=(moments,) * 3,
        check_vma=False,
    )
```

```python
import jax
import jax.numpy as jnp
from jax import lax
from jax.experimental import pallas as pl
from jax.experimental.pallas import tpu as pltpu
from jax.sharding import PartitionSpec as P

SUB = 2
MESH = pl.DeviceIdType.MESH
LEVELS, ROWS, LONS, REGIONS = 4, 8, 768, 22
LINE, HALF = 8, 384


def upwind(faces, left, right):
    forward = faces > 0.0
    mean, along, cross = (jnp.where(forward, l, r) for l, r in zip(left, right))
    weight = 0.5 * (jnp.where(forward, 1.0, -1.0) - faces)
    return faces * (mean + weight * along), faces * along, faces * cross


def advance(cells, flux, flux_next, mean_prev, mean_next):
    mean, along, cross = cells
    return (
        mean + (flux[0] - flux_next[0]),
        0.5 * (along + (flux[1] - flux_next[1])) + 0.25 * (mean_next - mean_prev),
        cross + (flux[2] - flux_next[2]),
    )


def zonal(cells, faces):
    count = faces.shape[-1]
    left = tuple(pltpu.roll(x, 1, 1) for x in cells)
    flux = upwind(faces, left, cells)
    flux_next = tuple(pltpu.roll(x, count - 1, 1) for x in flux)
    return advance(cells, flux, flux_next, left[0], pltpu.roll(cells[0], count - 1, 1))


def wind_of(winds, c, level):
    return jnp.concatenate([winds[c, 2 * level], winds[c, 2 * level + 1]], -1)


def step_kernel(
    mean_h, lon_h, lat_h, zon_h, mer_h, mix_h, flux_h, region_h, scaling_h, reader_h,
    cells,
    mix_v, flux_v, region_v, scaling_s, reader_s, slab, got_u, got_v, got_spare_u, got_spare_v, mine, theirs, slips, slips_in,
    winds, beyond, pack, halo, edge, south, last, north,
    in_sem, own_sem, scatter_send, scatter_recv, swap_send, swap_recv, slip_send, slip_recv, gather_send, gather_recv,
    halo_send, halo_recv, late, beside,
):
    band, me = lax.axis_index("band"), lax.axis_index("member")
    bands = lax.axis_size("band")
    line = (me // 2) % 2
    place = me // 4 * 2 + me % 2
    got = ((got_u, got_v), (got_spare_u, got_spare_v))
    has_south, has_north = band > 0, band < bands - 1
    around = has_south.astype(jnp.int32) + has_north.astype(jnp.int32)
    tail_end = me == 0
    answers = jnp.logical_and(tail_end, band % 2 == 0)
    owns = place != 0
    owns_spare = place == 1
    partner = me + 2 - 4 * line

    def member(where, which):
        return (where // 2 * 2 + which) * 2 + where % 2

    loads = [
        pltpu.make_async_copy(mix_h, mix_v, in_sem.at[3]),
        pltpu.make_async_copy(flux_h, flux_v, in_sem.at[4]),
        pltpu.make_async_copy(region_h, region_v, in_sem.at[5]),
        pltpu.make_async_copy(scaling_h, scaling_s, in_sem.at[6]),
        pltpu.make_async_copy(mean_h.at[0], cells.at[0], in_sem.at[0]),
        pltpu.make_async_copy(lon_h.at[0], cells.at[1], in_sem.at[1]),
        pltpu.make_async_copy(lat_h.at[0], cells.at[2], in_sem.at[2]),
    ]
    slab_loads = [
        pltpu.make_async_copy(zon_h.at[0], slab.at[0], in_sem.at[8]),
        pltpu.make_async_copy(mer_h.at[0], slab.at[1], in_sem.at[9]),
    ]
    load_reader = pltpu.make_async_copy(reader_h, reader_s, in_sem.at[7])

    def signal_beside(semaphore, who):
        for there, step in ((has_south, -1), (has_north, 1)):
            @pl.when(there)
            def _():
                pl.semaphore_signal(semaphore, inc=1, device_id=(band + step, who), device_id_type=MESH)

    def signal_line(semaphore):
        for step in range(1, LINE):
            target = member((place + step) % LINE, line)
            pl.semaphore_signal(semaphore, inc=1, device_id=(band, target), device_id_type=MESH)

    barrier = pltpu.get_barrier_semaphore()

    @pl.when(jnp.logical_not(tail_end))
    def _():
        signal_line(barrier)

    @pl.when(owns)
    def _():
        pl.semaphore_signal(barrier, inc=1, device_id=(band, partner), device_id_type=MESH)
        signal_beside(barrier, partner)

    pl.when(jnp.logical_not(answers))(lambda: signal_beside(barrier, me))
    def enter(tail_end_here):
        in_line = jnp.where(jnp.logical_and(line == 0, owns), LINE - 2, LINE - 1)
        outside = jnp.where(owns, 1 + 2 * around, jnp.where(jnp.logical_or(answers, me == 2), around, 0))
        pl.semaphore_wait(barrier, in_line + outside)

        def piece(c, there):
            field = (mer_h if c else zon_h).at[0] if tail_end_here else slab.at[c]
            return field.at[there // 2, :, pl.ds(pl.multiple_of(there % 2 * HALF, HALF), HALF)]

        for c in range(2):
            for step in (4, 5, 3, 2, 6, 7, 1, 0):
                there = (place + step) % LINE
                for spare in range(2):
                    def send():
                        pltpu.make_async_remote_copy(
                            src_ref=piece(c, there), dst_ref=got[spare][c].at[place], send_sem=scatter_send,
                            recv_sem=scatter_recv.at[spare, c], device_id=(band, member(jnp.maximum(there, 1), line)),
                            device_id_type=MESH,
                        ).start()

                    def keep():
                        pltpu.make_async_copy(piece(c, there), got[spare][c].at[place], own_sem.at[spare, c]).start()

                    fits = there == 0 if spare else there != 0
                    if step in (0, 7):
                        pl.when(jnp.logical_and(fits, jnp.maximum(there, 1) == place))(keep)
                        pl.when(jnp.logical_and(fits, jnp.maximum(there, 1) != place))(send)
                    else:
                        pl.when(fits)(send)

    for load in loads[:7]:
        load.start()

    @pl.when(tail_end)
    def _():
        enter(True)
        signal_line(late)

    pl.when(answers)(lambda: signal_beside(beside, me))

    @pl.when(jnp.logical_not(tail_end))
    def _():
        for load in slab_loads:
            load.start()

    load_reader.start()
    for load in loads[:4]:
        load.wait()
    region = region_v[...]
    weight = jnp.zeros(region.shape, jnp.float32)
    for code in range(REGIONS):
        weight = jnp.where(region == code, scaling_s[0, code], weight)
    land = jnp.where(region < REGIONS // 2, 1.0, 0.4)
    emission = 0.5 * flux_v[...] * land * weight
    zero = jnp.zeros_like(emission)
    below = [zero] + [mix_v[level] for level in range(LEVELS - 1)]
    above = below[1:] + [zero]
    ratios, inverse = [], []
    for level in range(LEVELS):
        denom = 1.0 + below[level] + above[level]
        if level:
            denom = denom + below[level] * ratios[-1]
        inverse.append(1.0 / denom)
        ratios.append(-above[level] * inverse[-1])
    for load in loads[4:]:
        load.wait()
    for k in range(3):
        values = []
        for level in range(LEVELS):
            source = cells[k, level]
            if k == 0 and level == 0:
                source = source + emission
            if level:
                source = source + below[level] * values[-1]
            values.append(source * inverse[level])
        result = values[-1]
        for level in range(LEVELS - 1, -1, -1):
            if level < LEVELS - 1:
                result = values[level] - ratios[level] * result
            cells[k, level] = result
            pack[0, k, pl.ds(2 * level, 2), :] = result[:2]
            pack[1, k, pl.ds(2 * level, 2), :] = result[ROWS - 2:]


    @pl.when(jnp.logical_not(tail_end))
    def _():
        for load in slab_loads:
            load.wait()
        enter(False)

    def across(side):
        return pltpu.make_async_remote_copy(
            src_ref=pack.at[side], dst_ref=halo.at[1 - side, pl.ds(0, 3)],
            send_sem=halo_send.at[side], recv_sem=halo_recv.at[1 - side],
            device_id=(band + (1 if side else -1), me), device_id_type=MESH,
        )

    sides = ((0, has_south), (1, has_north))

    load_reader.wait()

    @pl.when(jnp.logical_and(tail_end, jnp.logical_not(answers)))
    def _():
        pl.semaphore_wait(beside, around)

    for side, there in sides:
        pl.when(there)(across(side).start)

    def arrive(spare, c):
        kept = got[spare][c].at[place]
        pltpu.make_async_copy(kept, kept, own_sem.at[spare, c]).wait()
        part = got[spare][c].at[pl.ds(0, LINE - 1)]
        pltpu.make_async_copy(part, part, scatter_recv.at[spare, c]).wait()

    reader = reader_s[0]
    here = (reader // 2) % 2 == line
    reader_place = reader // 4 * 2 + reader % 2

    def swap(spare, c):
        return pltpu.make_async_remote_copy(
            src_ref=mine.at[spare, c], dst_ref=theirs.at[spare, c], send_sem=swap_send.at[spare, c],
            recv_sem=swap_recv.at[spare, c], device_id=(band, partner), device_id_type=MESH,
        )

    def slip(spare, c, side, other):
        return pltpu.make_async_remote_copy(
            src_ref=slips.at[spare, c, side], dst_ref=slips_in.at[spare, c, 1 - side, other],
            send_sem=slip_send.at[spare, c, side, other], recv_sem=slip_recv.at[spare, c, 1 - side, other],
            device_id=(band + (1 if side else -1), partner if other else me), device_id_type=MESH,
        )

    def offer(spare, c):
        chosen = got[spare][c][reader_place]
        mine[spare, c] = chosen
        swap(spare, c).start()
        slips[spare, c, 0] = jnp.where(here, chosen[:2], 0.0)
        slips[spare, c, 1] = jnp.where(here, chosen[ROWS - 2:], 0.0)
        for side, there in sides:
            for other in (1, 0):
                pl.when(there)(slip(spare, c, side, other).start)

    def share(ref, part, c, whose):
        for step in (4, 5, 3, 2, 6, 7, 1):
            target = member((place + step) % LINE, line)
            pltpu.make_async_remote_copy(
                src_ref=ref.at[c, whose], dst_ref=ref.at[c, whose], send_sem=gather_send.at[part, c],
                recv_sem=gather_recv.at[part, c], device_id=(band, target), device_id_type=MESH,
            ).start()

    def settle(spare, c):
        swap(spare, c).wait_recv()
        whose = 0 if spare else place
        winds[c, whose] = jnp.where(here, mine[spare, c], theirs[spare, c])
        share(winds, 0, c, whose)

    def settle_beside(spare, c):
        whose = 0 if spare else place
        for side, there in sides:
            @pl.when(there)
            def _():
                for other in range(2):
                    slip(spare, c, 1 - side, other).wait_recv()
                both = slips_in[spare, c, side, 0] + slips_in[spare, c, side, 1]
                beyond[c, whose, pl.ds(2 * side, 2), :] = both

            @pl.when(jnp.logical_not(there))
            def _():
                beyond[c, whose, pl.ds(2 * side, 2), :] = jnp.zeros((2, HALF), jnp.float32)

        share(beyond, 1, c, whose)

    @pl.when(owns)
    def _():
        for c in range(2):
            arrive(0, c)
            offer(0, c)

            @pl.when(owns_spare)
            def _():
                arrive(1, c)
                offer(1, c)

        @pl.when(line == 0)
        def _():
            pl.semaphore_wait(late, 1)

        for c in range(2):
            settle(0, c)
            pl.when(owns_spare)(lambda: settle(1, c))
            settle_beside(0, c)
            pl.when(owns_spare)(lambda: settle_beside(1, c))

    def await_winds(ref, part, c):
        cases = ((0, jnp.logical_not(owns)), (1, jnp.logical_and(owns, jnp.logical_not(owns_spare))), (2, owns_spare))
        for owned, case in cases:
            @pl.when(case)
            def _():
                some = ref.at[c, pl.ds(0, LINE - owned)]
                pltpu.make_async_copy(some, some, gather_recv.at[part, c]).wait()

    def halo_wind(c):
        await_winds(beyond, 1, c)
        for there in range(LINE):
            for side in range(2):
                place_rows = (pl.ds(there // 2 * 2, 2), pl.ds(there % 2 * HALF, HALF))
                halo[side, 3 + c, *place_rows] = beyond[c, there, pl.ds(2 * side, 2), :]

    row = lax.broadcasted_iota(jnp.int32, (ROWS, LONS), 0)
    order = (0, 2, 1)

    def up(x):
        return pltpu.roll(x, 1, 0)

    def down(x):
        return pltpu.roll(x, ROWS - 1, 0)

    def meridional(c):
        return (c[0], c[2], c[1])

    no_south, no_north = jnp.logical_not(has_south), jnp.logical_not(has_north)
    for sub in range(SUB):
        if sub == 0:
            await_winds(winds, 0, 0)
        for level in range(LEVELS):
            swept = zonal(tuple(cells[k, level] for k in range(3)), wind_of(winds, 0, level))
            for k in range(3):
                cells[k, level] = swept[k]
                edge[k, pl.ds(2 * level, 1), :] = swept[k][ROWS - 1:]
                edge[k, pl.ds(2 * level + 1, 1), :] = swept[k][:1]
        if sub == 0:
            for side, there in sides:
                @pl.when(there)
                def _():
                    across(1 - side).wait_recv()

                @pl.when(jnp.logical_not(there))
                def _():
                    halo[side, pl.ds(0, 3)] = jnp.zeros((3, ROWS, LONS), jnp.float32)

            halo_wind(0)
            s_cells = tuple(halo[0, k] for k in range(3))
            n_cells = tuple(halo[1, k] for k in range(3))
        edges = tuple(edge[k] for k in range(3))
        s_cells = tuple(jnp.where(no_south, e, x) for e, x in zip(edges, zonal(s_cells, halo[0, 3])))
        n_cells = tuple(jnp.where(no_north, e, x) for e, x in zip(edges, zonal(n_cells, halo[1, 3])))
        s_mer, n_mer, e_mer = meridional(s_cells), meridional(n_cells), meridional(edges)
        if sub == 0:
            await_winds(winds, 0, 1)
            halo_wind(1)
            v_north = jnp.where(no_north, 0.0, halo[1, 4])
            for level in range(LEVELS):
                edge[3, pl.ds(2 * level + 1, 1), :] = wind_of(winds, 1, level)[:1]
                edge[3, pl.ds(2 * level, 1), :] = jnp.zeros((1, LONS), jnp.float32)
        flux_8 = upwind(v_north, e_mer, n_mer)
        for k in range(3):
            south[k] = s_mer[k]
            last[k] = flux_8[k]
        north[...] = n_cells[0]
        if sub < SUB - 1:
            flux_m1 = upwind(halo[0, 4], tuple(up(x) for x in s_mer), s_mer)
            flux_0 = upwind(edge[3], s_mer, e_mer)
            s_cells = meridional(advance(s_mer, flux_m1, flux_0, up(s_mer[0]), e_mer[0]))
            flux_9 = upwind(down(v_north), n_mer, tuple(down(x) for x in n_mer))
            n_cells = meridional(advance(n_mer, flux_8, flux_9, e_mer[0], down(n_mer[0])))
        for level in range(LEVELS):
            faces = jnp.where(jnp.logical_and(row == 0, no_south), 0.0, wind_of(winds, 1, level))
            now = tuple(cells[k, level] for k in order)
            left = tuple(
                jnp.where(row == 0, south[k, pl.ds(2 * level + 1, 1), :], up(x)) for k, x in enumerate(now)
            )
            flux = upwind(faces, left, now)
            flux_next = tuple(
                jnp.where(row == ROWS - 1, last[k, pl.ds(2 * level, 1), :], down(x)) for k, x in enumerate(flux)
            )
            mean_next = jnp.where(row == ROWS - 1, north[pl.ds(2 * level, 1), :], down(now[0]))
            new = advance(now, flux, flux_next, left[0], mean_next)
            for k, value in zip(order, new):
                cells[k, level] = value

    def drain(ref, count, semaphore):
        some = ref.at[pl.ds(0, count)]
        pltpu.make_async_copy(some, some, semaphore).wait()

    def drain_owner(spare, c):
        swap(spare, c).wait_send()
        for side, there in sides:
            for other in range(2):
                pl.when(there)(slip(spare, c, side, other).wait_send)
        for part, ref in enumerate((winds, beyond)):
            drain(ref.at[c], LINE - 1, gather_send.at[part, c])

    for c in range(2):
        drain(got_u, LINE - 2, scatter_send)
        pl.when(jnp.logical_not(owns))(lambda: drain(got_u, 2, scatter_send))

        @pl.when(owns)
        def _():
            drain_owner(0, c)
            pl.when(owns_spare)(lambda: drain_owner(1, c))
            pl.when(jnp.logical_not(owns_spare))(lambda: drain(got_u, 1, scatter_send))

    for side, there in sides:
        pl.when(there)(across(side).wait_send)


def store_kernel(cells, out_mean, out_lon, out_lat, out_sem):
    stores = [
        pltpu.make_async_copy(cells.at[k], out.at[0], out_sem.at[k]) for k, out in enumerate((out_mean, out_lon, out_lat))
    ]
    for store in stores:
        store.start()
    for store in stores:
        store.wait()


def on_device(*args):
    hbm = pl.BlockSpec(memory_space=pl.ANY)
    local = pl.BlockSpec(memory_space=pltpu.VMEM)
    dma, regular = pltpu.SemaphoreType.DMA, pltpu.SemaphoreType.REGULAR

    def vmem(*dims):
        return pltpu.VMEM(dims, jnp.float32)

    cells = pl.pallas_call(
        step_kernel,
        out_shape=vmem(3, LEVELS, ROWS, LONS),
        in_specs=[hbm] * 10,
        out_specs=local,
        scratch_shapes=[
            vmem(LEVELS - 1, ROWS, LONS),
            vmem(ROWS, LONS),
            pltpu.VMEM((ROWS, LONS), jnp.int32),
            pltpu.SMEM((1, REGIONS), jnp.float32),
            pltpu.SMEM((1,), jnp.int32),
            vmem(2, LEVELS, ROWS, LONS),
            *[vmem(LINE, ROWS, HALF)] * 4,
            vmem(2, 2, ROWS, HALF),
            vmem(2, 2, ROWS, HALF),
            vmem(2, 2, 2, 2, HALF),
            vmem(2, 2, 2, 2, 2, HALF),
            vmem(2, LINE, ROWS, HALF),
            vmem(2, LINE, 4, HALF),
            vmem(2, 3, ROWS, LONS),
            vmem(2, 5, ROWS, LONS),
            vmem(4, ROWS, LONS),
            vmem(3, ROWS, LONS),
            vmem(3, ROWS, LONS),
            vmem(ROWS, LONS),
            dma((10,)), dma((2, 2)), dma, dma((2, 2)), dma((2, 2)), dma((2, 2)), dma((2, 2, 2, 2)), dma((2, 2, 2, 2)),
            dma((2, 2)), dma((2, 2)), dma((2,)), dma((2,)), regular, regular,
        ],
        compiler_params=pltpu.CompilerParams(collective_id=0, has_side_effects=True),
    )(*args)
    return pl.pallas_call(
        store_kernel,
        out_shape=(jax.ShapeDtypeStruct(args[0].shape, jnp.float32),) * 3,
        in_specs=[local],
        out_specs=(hbm,) * 3,
        scratch_shapes=[dma((3,))],
    )(pltpu.with_memory_space_constraint(cells, pltpu.VMEM))


def solution(mesh):
    moments = P("member", None, "band", None)
    return jax.shard_map(
        on_device,
        mesh=mesh,
        in_specs=(
            moments, moments, moments, moments, moments,
            P(None, "band", None),
            P("band", None),
            P("band", None),
            P("member", None),
            P("band"),
        ),
        out_specs=(moments,) * 3,
        check_vma=False,
    )
```
